32 devices in a mesh: groups: 2 (over y), chan: 8 (over z, x), pair: 2 (over core).
Axes of the slice: x: 2, y: 2, z: 4, core: 2. Of those that a mesh axis runs over, the one named last changes fastest.
Arguments:
- raw: bfloat16 [1024, 1, 12000], P(('groups', 'chan')), parts along dimension 0, may hold values from -6 to 6
- live_index: int32 [16, 64], P(('groups', 'chan')), parts along dimension 0, may hold values from 0 to 63, each once within a row
- live_count: int32 [16], P('groups'), parts along dimension 0, may hold values from 1 to 64, 256 in all
Outputs:
- correlation: bfloat16 [6, 1024, 512], P('pair', ('groups', 'chan')), parts along dimension 1
The draws below stay inside these ranges and needn't reach their ends.
There are 2 independent parts, one for each index of `groups`. The reference program is written for one: setup_inputs(seed, part) draws one part's arguments, and reference() takes and returns one part's arrays. A program takes and returns all parts, laid end to end along the dimension named above; each array names one. Nothing has to cross between parts.
Inputs may be any that keep to these rules, and one draw needn't show every extreme that they name: `live_index`: each block's row is a permutation of the raw channels of that block. `live_count`: live slots of each block; they sum to 256, and some block fills all 64 slots.
All inputs are finite; a program needn't handle non-finite values.
Results may differ from the reference program's by a relative error of at most 0.001.
The reference program's roundings to bfloat16 on the way (of `picked`, `dft_table`, `whitened` and `weighted`) count: a program that leaves them out, or rounds other values in their place, can miss the bound.
Values may be sent and summed in bfloat16 or wider, within the bound.
No kernel may reach another device: no remote copies, remote signals or barrier semaphores. Data moves between devices by JAX's collectives and lax.ppermute only.
A program may use at most 128 MiB of HBM per device.

```python
import math
import jax
import jax.numpy as jnp
import numpy as np
from jax import lax

S = 12000
NB = 448
NSEG = 1
L = 6
LSTEP = 125
F0 = 60
CAP = 64
BLOCKS = 8
SLOTS = 512
LIVE = 256


def level_of(own_key, extent, pieces, least, high):
    gain = 1.0
    for position, shards_of in pieces:
        steps = jax.random.uniform(jax.random.fold_in(jax.random.fold_in(own_key, 6), position), (shards_of,), jnp.float32, least / len(pieces), high / len(pieces))
        gain = gain * jnp.repeat(jnp.exp(steps), extent[position] // shards_of).reshape((-1,) + (1,) * (len(extent) - 1 - position))
    return gain


def split_up(amount, total, most, lean):
    loads = [(1 << 20) // math.isqrt(grade ** lean) + 1 for grade in range(2, amount + 1)]
    spare, holding = total - most - (amount - 1), [1] * (amount - 1)
    while spare > 0:
        candidates = [i for i in range(amount - 1) if holding[i] < most]
        whole, budget = sum([loads[i] for i in candidates]), spare
        for i in candidates:
            extra = min(most - holding[i], max(1, budget * loads[i] // whole), spare)
            holding[i] = holding[i] + extra
            spare = spare - extra
    return np.array([most] + holding)


def uneven_parts(rng, count, total, bound, lean):
    if count == 2:
        one = jax.random.randint(rng, (), max(1, total - bound), min(bound, total - 1) + 1)
        return jnp.stack([one, total - one])
    lengths = jnp.asarray(split_up(count, total, bound, lean), jnp.int32)
    twos = (count - 1) // 2
    source_of, receiver = lengths[1:1 + 2 * twos:2], lengths[2:2 + 2 * twos:2]
    slack = jnp.minimum(source_of - 1, bound - receiver)
    passed = jax.random.randint(jax.random.fold_in(rng, 1), (twos,), 0, 1 << 20) % (slack + 1)
    lengths = lengths.at[1:1 + 2 * twos:2].set(source_of - passed).at[2:2 + 2 * twos:2].set(receiver + passed)
    return lengths[jax.random.permutation(jax.random.fold_in(rng, 2), count)]


def gaussian(key, shape, spread, reach, pieces=(), held_as=jnp.bfloat16):
    drawn = jax.random.normal(key, shape, jnp.float32) * spread
    if len(pieces) > 0:
        drawn = level_of(key, shape, pieces, -0.22, 0.18) * drawn
    return jnp.clip(drawn, min=-reach, max=reach).astype(held_as)


def setup_inputs(seed: int = 0, part: int = 0) -> dict:
    key_list = jax.random.split(jax.random.key(seed), 4)
    part_splits = jax.random.split(jax.random.fold_in(key_list[3], part), 4)
    raw = gaussian(part_splits[0], (SLOTS, NSEG, S), 1.0, 6.0, ((0, 8),))
    live_index = jax.vmap(lambda own: jax.random.permutation(own, CAP))(jax.random.split(part_splits[1], BLOCKS)).reshape((BLOCKS, CAP)).astype(jnp.int32)
    live_count = uneven_parts(part_splits[2], BLOCKS, LIVE, CAP, 2).astype(jnp.int32)
    return dict(raw=raw, live_index=live_index, live_count=live_count)


water_level = 0.1

def lag_weights(lag_ids, bin_ids):
    band_taper = 0.5 - 0.5 * jnp.cos(2.0 * jnp.pi * (bin_ids.astype(jnp.float32) + 0.5) / NB)
    phase_int = (F0 + bin_ids)[None, :] * lag_ids[:, None] % S
    waves = jnp.cos(phase_int.astype(jnp.float32) * (2.0 * jnp.pi / S))
    return band_taper[None, :] * waves / jnp.sqrt(jnp.float32(NSEG * NB))

def reference(raw, live_index, live_count):
    blocks = live_count.shape[0]
    raw_rows = (jnp.arange(blocks, dtype=jnp.int32)[:, None] * CAP + live_index).reshape(-1).astype(jnp.int32)
    live_mask = (jnp.arange(CAP, dtype=jnp.int32)[None, :] < live_count[:, None]).reshape(-1)
    picked = jnp.where(live_mask[:, None, None], raw[raw_rows], jnp.zeros((), raw.dtype))
    sample_ids = jnp.arange(S, dtype=jnp.int32)
    bin_ids = jnp.arange(NB, dtype=jnp.int32)
    phase_int = sample_ids[:, None] * (F0 + bin_ids)[None, :] % S
    angles = phase_int.astype(jnp.float32) * (2.0 * jnp.pi / S)
    dft_table = jnp.concatenate([jnp.cos(angles), -jnp.sin(angles)], axis=1).astype(jnp.bfloat16)
    spectrum = jnp.dot(picked.reshape(-1, S), dft_table, preferred_element_type=jnp.float32)
    spectrum = spectrum.reshape(SLOTS, NSEG, 2, NB)
    band_power = lax.optimization_barrier(jnp.sum(spectrum * spectrum, axis=(2, 3))) / NB
    magnitude = spectrum[:, :, 0] ** 2 + spectrum[:, :, 1] ** 2
    denom = jnp.sqrt(magnitude + water_level * band_power[:, :, None] + 1e-06)
    whitened = (spectrum / denom[:, :, None, :]).astype(jnp.bfloat16)
    flat_spectra = whitened.reshape(SLOTS, -1)
    lag_ids = (jnp.arange(L, dtype=jnp.int32) * LSTEP).astype(jnp.int32)
    weights = lag_weights(lag_ids, bin_ids)

    def per_lag(weight_row):
        weighted = (whitened.astype(jnp.float32) * weight_row[None, None, None, :]).astype(jnp.bfloat16)
        product = lax.dot_general(weighted.reshape(SLOTS, -1), flat_spectra, (((1,), (1,)), ((), ())), preferred_element_type=jnp.float32)
        return product.astype(jnp.bfloat16)
    return lax.map(per_lag, weights)
```

```python
import functools

import jax
import jax.numpy as jnp
import numpy as np
from jax import lax
from jax.experimental import pallas as pl
from jax.experimental.pallas import tpu as pltpu
from jax.sharding import PartitionSpec as P

S = 12000
NB = 448
NSEG = 1
L = 6
LSTEP = 125
F0 = 60

water_level = 0.1

QUARTER = S // 4
CHUNK = 256
CHUNKS = -(-QUARTER // CHUNK)
DEPTH = CHUNKS * CHUNK
GROUP = 4
RES = (0, 2, 1, 3)
PER = NB // 4
LANES = 128
SPARE = LANES - PER
WIDTH = 2 * NB


def bins_of(residue):
    return np.arange(residue, NB, 4)


def quarter_table():
    table = np.zeros((DEPTH, 8 * LANES), np.float32)
    t = np.arange(QUARTER, dtype=np.int64)
    for place, residue in enumerate(RES):
        phase = t[:, None] * (F0 + bins_of(residue))[None, :] % S
        angles = phase.astype(np.float32) * np.float32(2.0 * np.pi / S)
        at = 2 * place * LANES
        table[:QUARTER, at : at + PER] = np.cos(angles.astype(np.float64))
        table[:QUARTER, at + LANES : at + LANES + PER] = -np.sin(angles.astype(np.float64))
    return table.astype(jnp.bfloat16)


def packed_bins():
    pieces = [bins_of(residue) for residue in RES for _ in range(2)]
    columns = []
    for p in range(7):
        columns.append(pieces[p])
        columns.append(pieces[7][p * SPARE : (p + 1) * SPARE])
    return np.concatenate(columns)


def lag_table():
    bins = packed_bins()
    taper = np.float32(0.5) - np.float32(0.5) * np.cos(
        np.float32(2.0 * np.pi) * (bins.astype(np.float32) + np.float32(0.5)) / np.float32(NB)
    )
    phase = (F0 + bins)[None, :] * (np.arange(L) * LSTEP)[:, None] % S
    waves = np.cos(phase.astype(np.float32) * np.float32(2.0 * np.pi / S))
    return (taper[None, :] * waves / np.sqrt(np.float32(NSEG * NB))).astype(np.float32)


def split(value):
    high = value.astype(jnp.bfloat16)
    low = (value - high.astype(jnp.float32)).astype(jnp.bfloat16)
    return high, low


def spectra_kernel(count_ref, index_ref, raw_ref, table_ref, out_ref, x, tail, table, y_even, y_half, y_odd, sems):
    rows = x.shape[0]
    whole = S // LANES * LANES
    x_copy = pltpu.make_async_copy(raw_ref, x, sems.at[0])
    x_copy.start()
    copies = []
    for g in range(CHUNKS // GROUP):
        span = pl.ds(g * GROUP * CHUNK, GROUP * CHUNK)
        copies.append(pltpu.make_async_copy(table_ref.at[span, :], table.at[span, :], sems.at[1 + g]))
        copies[-1].start()
    tail[...] = jnp.zeros_like(tail)
    x_copy.wait()
    tail[:, : S - whole] = x[:, whole:S]

    def window(start):
        base = start // LANES * LANES
        shift = start - base
        parts = []
        for lane in range(base, base + CHUNK + (LANES if shift else 0), LANES):
            if lane + LANES <= S:
                parts.append(x[:, lane : lane + LANES])
            elif lane < S:
                parts.append(tail[...])
            else:
                parts.append(jnp.zeros((rows, LANES), x.dtype))
        value = jnp.concatenate(parts, axis=1).astype(jnp.float32)
        if shift:
            value = pltpu.roll(value, value.shape[1] - shift, axis=1)[:, :CHUNK]
        return value

    even = jnp.zeros((2 * rows, 2 * LANES), jnp.float32)
    half = jnp.zeros((2 * rows, 2 * LANES), jnp.float32)
    odd = jnp.zeros((4 * rows, 4 * LANES), jnp.float32)
    for g in range(CHUNKS // GROUP):
        for c in range(g * GROUP, (g + 1) * GROUP):
            at = c * CHUNK
            x0, x1, x2, x3 = (window(m * QUARTER + at) for m in range(4))
            sum02, sum13 = x0 + x2, x1 + x3
            for target, first, value in (
                (y_even, 0, sum02 + sum13),
                (y_half, 0, sum02 - sum13),
                (y_odd, 0, x0 - x2),
                (y_odd, 2 * rows, x1 - x3),
            ):
                high, low = split(value)
                target[first : first + rows, at : at + CHUNK] = high
                target[first + rows : first + 2 * rows, at : at + CHUNK] = low
        copies[g].wait()
        lo, hi = g * GROUP * CHUNK, (g + 1) * GROUP * CHUNK
        even += jnp.dot(y_even[:, lo:hi], table[lo:hi, : 2 * LANES], preferred_element_type=jnp.float32)
        half += jnp.dot(y_half[:, lo:hi], table[lo:hi, 2 * LANES : 4 * LANES], preferred_element_type=jnp.float32)
        odd += jnp.dot(y_odd[:, lo:hi], table[lo:hi, 4 * LANES :], preferred_element_type=jnp.float32)

    even = even[:rows] + even[rows:]
    half = half[:rows] + half[rows:]
    u = odd[:rows] + odd[rows : 2 * rows]
    v = odd[2 * rows : 3 * rows] + odd[3 * rows :]
    pairs = (
        (even[:, :LANES], even[:, LANES:]),
        (half[:, :LANES], half[:, LANES:]),
        (u[:, :LANES] + v[:, LANES : 2 * LANES], u[:, LANES : 2 * LANES] - v[:, :LANES]),
        (u[:, 2 * LANES : 3 * LANES] - v[:, 3 * LANES :], u[:, 3 * LANES :] + v[:, 2 * LANES : 3 * LANES]),
    )
    power = [re * re + im * im for re, im in pairs]
    band_power = jnp.sum(power[0] + power[1] + power[2] + power[3], axis=1, keepdims=True) / NB
    pieces = []
    for (re, im), own in zip(pairs, power):
        denom = jnp.sqrt(own + water_level * band_power + 1e-06)
        pieces += [re / denom, im / denom]
    lanes = lax.broadcasted_iota(jnp.int32, (rows, LANES), 1)
    packed = []
    for p in range(7):
        moved = pltpu.roll(pieces[7], (PER - p * SPARE) % LANES, axis=1)
        packed.append(jnp.where(lanes < PER, pieces[p], moved))
    whitened = jnp.concatenate(packed, axis=1).astype(jnp.bfloat16)
    source = lax.broadcasted_iota(jnp.int32, (rows, rows), 0)
    slot = lax.broadcasted_iota(jnp.int32, (rows, rows), 1)
    chosen = jnp.logical_and(source == index_ref[...], slot < count_ref[0])
    pick = jnp.where(chosen, 1.0, 0.0).astype(jnp.bfloat16)
    out_ref[...] = lax.dot_general(
        pick, whitened, (((0,), (0,)), ((), ())), preferred_element_type=jnp.float32
    ).astype(jnp.bfloat16)


def spectra(raw_rows, index_row, count, table):
    rows = raw_rows.shape[0]
    return pl.pallas_call(
        spectra_kernel,
        out_shape=jax.ShapeDtypeStruct((rows, WIDTH), jnp.bfloat16),
        in_specs=[
            pl.BlockSpec(memory_space=pltpu.SMEM),
            pl.BlockSpec(memory_space=pltpu.VMEM),
            pl.BlockSpec(memory_space=pl.ANY),
            pl.BlockSpec(memory_space=pl.ANY),
        ],
        out_specs=pl.BlockSpec(memory_space=pltpu.VMEM),
        scratch_shapes=[
            pltpu.VMEM((rows, S), jnp.bfloat16),
            pltpu.VMEM((rows, LANES), jnp.bfloat16),
            pltpu.VMEM((DEPTH, 8 * LANES), jnp.bfloat16),
            pltpu.VMEM((2 * rows, DEPTH), jnp.bfloat16),
            pltpu.VMEM((2 * rows, DEPTH), jnp.bfloat16),
            pltpu.VMEM((4 * rows, DEPTH), jnp.bfloat16),
            pltpu.SemaphoreType.DMA((1 + CHUNKS // GROUP,)),
        ],
        compiler_params=pltpu.CompilerParams(vmem_limit_bytes=40 * 1024 * 1024),
        cost_estimate=pl.CostEstimate(
            flops=2 * DEPTH * rows * 3072, bytes_accessed=DEPTH * 2048 + rows * S * 2, transcendentals=0
        ),
        name="spectra",
    )(count, index_row, raw_rows, table)


def correlate(lag_rows, columns):
    product = lax.dot_general(
        lag_rows, columns, (((1,), (1,)), ((), ())), preferred_element_type=jnp.float32
    )
    return product.astype(jnp.bfloat16)


def shards(table, weights, raw, live_index, live_count):
    slot_count, seg_count, samples = raw.shape
    pair_index = lax.axis_index("pair")
    lag_share = L // lax.axis_size("pair")
    count = lax.dynamic_slice_in_dim(live_count, lax.axis_index("chan"), 1)
    own = spectra(raw.reshape(slot_count * seg_count, samples), live_index, count, table)
    own_weights = lax.dynamic_slice_in_dim(weights, pair_index * lag_share, lag_share, 0)
    lag_rows = (own.astype(jnp.float32)[None] * own_weights[:, None, :]).astype(jnp.bfloat16)
    lag_rows = lag_rows.reshape(lag_share * slot_count, -1)
    product = correlate(lag_rows, lax.all_gather(own, "chan", axis=0, tiled=True))
    return product.reshape(lag_share, slot_count, -1)


def solution(mesh):
    local = functools.partial(shards, jnp.asarray(quarter_table()), jnp.asarray(lag_table()))
    return jax.shard_map(
        local,
        mesh=mesh,
        in_specs=(P(("groups", "chan"), None, None), P(("groups", "chan"), None), P("groups")),
        out_specs=P("pair", ("groups", "chan"), None),
        check_vma=False,
    )
```

```python
import functools

import jax
import jax.numpy as jnp
import numpy as np
from jax import lax
from jax.experimental import pallas as pl
from jax.experimental.pallas import tpu as pltpu
from jax.sharding import PartitionSpec as P

S = 12000
NB = 448
NSEG = 1
L = 6
LSTEP = 125
F0 = 60

water_level = 0.1

QUARTER = S // 4
CHUNK = 256
CHUNKS = -(-QUARTER // CHUNK)
DEPTH = CHUNKS * CHUNK
GROUP = 2
RES = (0, 2, 1, 3)
PER = NB // 4
LANES = 128
SPARE = LANES - PER
WIDTH = 2 * NB
VMEM_MIB = 60


def bins_of(residue):
    return np.arange(residue, NB, 4)


def quarter_table():
    table = np.zeros((DEPTH, 8 * LANES), np.float32)
    t = np.arange(QUARTER, dtype=np.int64)
    for place, residue in enumerate(RES):
        phase = t[:, None] * (F0 + bins_of(residue))[None, :] % S
        angles = phase.astype(np.float32) * np.float32(2.0 * np.pi / S)
        at = 2 * place * LANES
        table[:QUARTER, at : at + PER] = np.cos(angles.astype(np.float64))
        table[:QUARTER, at + LANES : at + LANES + PER] = -np.sin(angles.astype(np.float64))
    return table.astype(jnp.bfloat16)


def packed_bins():
    pieces = [bins_of(residue) for residue in RES for _ in range(2)]
    columns = []
    for p in range(7):
        columns.append(pieces[p])
        columns.append(pieces[7][p * SPARE : (p + 1) * SPARE])
    return np.concatenate(columns)


def lag_table():
    bins = packed_bins()
    taper = np.float32(0.5) - np.float32(0.5) * np.cos(
        np.float32(2.0 * np.pi) * (bins.astype(np.float32) + np.float32(0.5)) / np.float32(NB)
    )
    phase = (F0 + bins)[None, :] * (np.arange(L) * LSTEP)[:, None] % S
    waves = np.cos(phase.astype(np.float32) * np.float32(2.0 * np.pi / S))
    return (taper[None, :] * waves / np.sqrt(np.float32(NSEG * NB))).astype(np.float32)


def split(value):
    high = value.astype(jnp.bfloat16)
    low = (value - high.astype(jnp.float32)).astype(jnp.bfloat16)
    return high, low


def spectra_kernel(
    lag_share,
    count_ref,
    index_ref,
    raw_ref,
    table_ref,
    weight_ref,
    out_ref,
    first_ref,
    second_ref,
    lag_ref,
    x,
    tail,
    table,
    y_even,
    y_half,
    y_odd,
    counts,
    index,
    weights,
    small_sems,
    sems,
):
    rows = x.shape[0]
    whole = S // LANES * LANES
    x_copy = pltpu.make_async_copy(raw_ref, x, sems.at[0])
    x_copy.start()
    count_copy = pltpu.make_async_copy(count_ref, counts, small_sems.at[0])
    index_copy = pltpu.make_async_copy(index_ref, index, small_sems.at[1])
    count_copy.start()
    index_copy.start()
    weight_copy = pltpu.make_async_copy(weight_ref.at[lax.axis_index("pair")], weights, small_sems.at[2])
    weight_copy.start()
    copies = []
    for g in range(CHUNKS // GROUP):
        span = pl.ds(g * GROUP * CHUNK, GROUP * CHUNK)
        copies.append(pltpu.make_async_copy(table_ref.at[span, :], table.at[span, :], sems.at[1 + g]))
        copies[-1].start()
    tail[...] = jnp.zeros_like(tail)
    x_copy.wait()
    tail[:, : S - whole] = x[:, whole:S]

    def window(start):
        base = start // LANES * LANES
        shift = start - base
        parts = []
        for lane in range(base, base + CHUNK + (LANES if shift else 0), LANES):
            if lane + LANES <= S:
                parts.append(x[:, lane : lane + LANES])
            elif lane < S:
                parts.append(tail[...])
            else:
                parts.append(jnp.zeros((rows, LANES), x.dtype))
        value = jnp.concatenate(parts, axis=1).astype(jnp.float32)
        if shift:
            value = pltpu.roll(value, value.shape[1] - shift, axis=1)[:, :CHUNK]
        return value

    even = jnp.zeros((2 * rows, 2 * LANES), jnp.float32)
    half = jnp.zeros((2 * rows, 2 * LANES), jnp.float32)
    odd = jnp.zeros((4 * rows, 4 * LANES), jnp.float32)
    for g in range(CHUNKS // GROUP):
        for c in range(g * GROUP, (g + 1) * GROUP):
            at = c * CHUNK
            x0, x1, x2, x3 = (window(m * QUARTER + at) for m in range(4))
            sum02, sum13 = x0 + x2, x1 + x3
            for target, first, value in (
                (y_even, 0, sum02 + sum13),
                (y_half, 0, sum02 - sum13),
                (y_odd, 0, x0 - x2),
                (y_odd, 2 * rows, x1 - x3),
            ):
                high, low = split(value)
                target[first : first + rows, at : at + CHUNK] = high
                target[first + rows : first + 2 * rows, at : at + CHUNK] = low
        copies[g].wait()
        lo, hi = g * GROUP * CHUNK, (g + 1) * GROUP * CHUNK
        even += jnp.dot(y_even[:, lo:hi], table[lo:hi, : 2 * LANES], preferred_element_type=jnp.float32)
        half += jnp.dot(y_half[:, lo:hi], table[lo:hi, 2 * LANES : 4 * LANES], preferred_element_type=jnp.float32)
        odd += jnp.dot(y_odd[:, lo:hi], table[lo:hi, 4 * LANES :], preferred_element_type=jnp.float32)

    even = even[:rows] + even[rows:]
    half = half[:rows] + half[rows:]
    u = odd[:rows] + odd[rows : 2 * rows]
    v = odd[2 * rows : 3 * rows] + odd[3 * rows :]
    pairs = (
        (even[:, :LANES], even[:, LANES:]),
        (half[:, :LANES], half[:, LANES:]),
        (u[:, :LANES] + v[:, LANES : 2 * LANES], u[:, LANES : 2 * LANES] - v[:, :LANES]),
        (u[:, 2 * LANES : 3 * LANES] - v[:, 3 * LANES :], u[:, 3 * LANES :] + v[:, 2 * LANES : 3 * LANES]),
    )
    power = [re * re + im * im for re, im in pairs]
    band_power = jnp.sum(power[0] + power[1] + power[2] + power[3], axis=1, keepdims=True) / NB
    pieces = []
    for (re, im), own in zip(pairs, power):
        denom = jnp.sqrt(own + water_level * band_power + 1e-06)
        pieces += [re / denom, im / denom]
    lanes = lax.broadcasted_iota(jnp.int32, (rows, LANES), 1)
    packed = []
    for p in range(7):
        moved = pltpu.roll(pieces[7], (PER - p * SPARE) % LANES, axis=1)
        packed.append(jnp.where(lanes < PER, pieces[p], moved))
    whitened = jnp.concatenate(packed, axis=1).astype(jnp.bfloat16)
    count_copy.wait()
    index_copy.wait()
    count = counts[lax.axis_index("chan")]
    source = lax.broadcasted_iota(jnp.int32, (rows, rows), 0)
    slot = lax.broadcasted_iota(jnp.int32, (rows, rows), 1)
    chosen = jnp.logical_and(source == index[...], slot < count)
    pick = jnp.where(chosen, 1.0, 0.0).astype(jnp.bfloat16)
    own = lax.dot_general(pick, whitened, (((0,), (0,)), ((), ())), preferred_element_type=jnp.float32)
    narrow = own.astype(jnp.bfloat16)
    out_ref[...] = narrow
    first_ref[...] = narrow[: rows // 2]
    second_ref[...] = narrow[rows // 2 :]
    weight_copy.wait()
    for lag in range(lag_share):
        lag_ref[lag * rows : (lag + 1) * rows, :] = (own * weights[lag : lag + 1, :]).astype(jnp.bfloat16)


def spectra(raw_rows, index_row, live_count, table, weights):
    rows = raw_rows.shape[0]
    lag_share = weights.shape[1]
    return pl.pallas_call(
        functools.partial(spectra_kernel, lag_share),
        out_shape=[
            jax.ShapeDtypeStruct((rows, WIDTH), jnp.bfloat16),
            jax.ShapeDtypeStruct((rows // 2, WIDTH), jnp.bfloat16),
            jax.ShapeDtypeStruct((rows // 2, WIDTH), jnp.bfloat16),
            jax.ShapeDtypeStruct((lag_share * rows, WIDTH), jnp.bfloat16),
        ],
        in_specs=[pl.BlockSpec(memory_space=pltpu.HBM)] * 5,
        out_specs=[pl.BlockSpec(memory_space=pltpu.VMEM)] * 4,
        scratch_shapes=[
            pltpu.VMEM((rows, S), jnp.bfloat16),
            pltpu.VMEM((rows, LANES), jnp.bfloat16),
            pltpu.VMEM((DEPTH, 8 * LANES), jnp.bfloat16),
            pltpu.VMEM((2 * rows, DEPTH), jnp.bfloat16),
            pltpu.VMEM((2 * rows, DEPTH), jnp.bfloat16),
            pltpu.VMEM((4 * rows, DEPTH), jnp.bfloat16),
            pltpu.SMEM(live_count.shape, jnp.int32),
            pltpu.VMEM(index_row.shape, jnp.int32),
            pltpu.VMEM(weights.shape[1:], jnp.float32),
            pltpu.SemaphoreType.DMA((3,)),
            pltpu.SemaphoreType.DMA((1 + CHUNKS // GROUP,)),
        ],
        compiler_params=pltpu.CompilerParams(vmem_limit_bytes=VMEM_MIB * 1024 * 1024),
        cost_estimate=pl.CostEstimate(
            flops=2 * DEPTH * rows * 3072, bytes_accessed=DEPTH * 2048 + rows * S * 2, transcendentals=0
        ),
        name="spectra",
    )(live_count, index_row, raw_rows, table, weights)


def correlate(lag_rows, columns):
    product = lax.dot_general(
        lag_rows, columns, (((1,), (1,)), ((), ())), preferred_element_type=jnp.float32
    )
    return product.astype(jnp.bfloat16)


def eight_kernel(lags, own, side, near, far, far_swap, near_swap, cross_a, cross_b, cross_swap_a, cross_swap_b, out):
    me = lax.axis_index("chan")
    core = lax.axis_index("pair")
    x, z = me % 2, me // 2
    rows = own.shape[0]
    upper = core == 1
    lag_rows = lags[...]
    tiles = (
        ((own[...], side[...]), z),
        (
            (
                jnp.where(upper, near_swap[...], near[...]),
                jnp.where(upper, near[...], near_swap[...]),
            ),
            z ^ 1,
        ),
        ((far[...], cross_swap_a[...], cross_swap_b[...]), z ^ (2 + core)),
        ((far_swap[...], cross_a[...], cross_b[...]), z ^ (3 - core)),
    )
    for blocks, plane in tiles:
        columns = jnp.concatenate(blocks, axis=0)
        product = lax.dot_general(
            lag_rows, columns, (((1,), (1,)), ((), ())), preferred_element_type=jnp.float32
        )
        product = jnp.where(x == 0, product, pltpu.roll(product, rows, axis=1)).astype(jnp.bfloat16)
        at = pl.multiple_of(plane * 2 * rows, 2 * rows)
        for lag in range(out.shape[0]):
            out[lag, :, pl.ds(at, 2 * rows)] = product[lag * rows : (lag + 1) * rows]


def exchange_eight(own, first, second, lags):
    def split_move(mask1, mask0):
        pairs = [(2 * c + 1, 2 * (c ^ mask1) + 1) for c in range(8)] + [(2 * c, 2 * (c ^ mask0)) for c in range(8)]
        return lambda a: lax.ppermute(a, ("chan", "pair"), pairs)

    def forward(a):
        pairs = [(2 * c + p, 2 * (c ^ 1) + 1 - p) for c in range(8) for p in range(2)]
        return lax.ppermute(a, ("chan", "pair"), pairs)

    def swap(a):
        return lax.ppermute(a, "pair", [(0, 1), (1, 0)])

    far_a = split_move(6, 4)(first)
    far_b = split_move(6, 4)(second)
    side = split_move(1, 1)(own)
    near = split_move(3, 2)(own)
    far_a_ready, side = lax.optimization_barrier((far_a, side))
    cross_a = forward(far_a_ready)
    cross_b = forward(far_b)
    far = jnp.concatenate([far_a, far_b], axis=0)
    far_swap, near_swap = swap(far), swap(near)
    cross_swap_a, cross_swap_b = swap(cross_a), swap(cross_b)
    lag_share, rows = lags.shape[0] // own.shape[0], own.shape[0]
    return pl.pallas_call(
        eight_kernel,
        out_shape=jax.ShapeDtypeStruct((lag_share, rows, 8 * rows), jnp.bfloat16),
        in_specs=[pl.BlockSpec(memory_space=pltpu.VMEM)] * 11,
        out_specs=pl.BlockSpec(memory_space=pltpu.VMEM),
        compiler_params=pltpu.CompilerParams(vmem_limit_bytes=32 * 1024 * 1024),
        cost_estimate=pl.CostEstimate(
            flops=2 * lag_share * rows * 8 * rows * WIDTH, bytes_accessed=12 * rows * WIDTH * 2, transcendentals=0
        ),
        name="correlate",
    )(lags, own, side, near, far, far_swap, near_swap, cross_a, cross_b, cross_swap_a, cross_swap_b)


def shards(table, weights, raw, live_index, live_count):
    slot_count, seg_count, samples = raw.shape
    pairs = lax.axis_size("pair")
    own, first, second, lags = spectra(
        raw.reshape(slot_count * seg_count, samples),
        live_index,
        live_count,
        table,
        weights.reshape(pairs, L // pairs, WIDTH),
    )
    if lax.axis_size("chan") == 8 and pairs == 2 and slot_count == 64:
        return exchange_eight(own, first, second, lags)
    product = correlate(lags, lax.all_gather(own, "chan", axis=0, tiled=True))
    return product.reshape(L // pairs, slot_count, -1)


def solution(mesh):
    local = functools.partial(shards, jnp.asarray(quarter_table()), jnp.asarray(lag_table()))
    return jax.shard_map(
        local,
        mesh=mesh,
        in_specs=(P(("groups", "chan"), None, None), P(("groups", "chan"), None), P("groups")),
        out_specs=P("pair", ("groups", "chan"), None),
        check_vma=False,
    )
```

```python
import functools

import jax
import jax.numpy as jnp
import numpy as np
from jax import lax
from jax.experimental import pallas as pl
from jax.experimental.pallas import tpu as pltpu
from jax.sharding import PartitionSpec as P

S = 12000
NB = 448
NSEG = 1
L = 6
LSTEP = 125
F0 = 60

water_level = 0.1

QUARTER = S // 4
CHUNK = 256
CHUNKS = -(-QUARTER // CHUNK)
DEPTH = CHUNKS * CHUNK
GROUP = 2
RES = (0, 2, 1, 3)
PER = NB // 4
LANES = 128
SPARE = LANES - PER
WIDTH = 2 * NB
VMEM_KIB = 40 * 1024
CORR_KIB = 32 * 1024


def bins_of(residue):
    return np.arange(residue, NB, 4)


def quarter_table():
    table = np.zeros((DEPTH, 8 * LANES), np.float32)
    t = np.arange(QUARTER, dtype=np.int64)
    for place, residue in enumerate(RES):
        phase = t[:, None] * (F0 + bins_of(residue))[None, :] % S
        angles = phase.astype(np.float32) * np.float32(2.0 * np.pi / S)
        at = 2 * place * LANES
        table[:QUARTER, at : at + PER] = np.cos(angles.astype(np.float64))
        table[:QUARTER, at + LANES : at + LANES + PER] = -np.sin(angles.astype(np.float64))
    return table.astype(jnp.bfloat16)


def packed_bins():
    pieces = [bins_of(residue) for residue in RES for _ in range(2)]
    columns = []
    for p in range(7):
        columns.append(pieces[p])
        columns.append(pieces[7][p * SPARE : (p + 1) * SPARE])
    return np.concatenate(columns)


def lag_table():
    bins = packed_bins()
    taper = np.float32(0.5) - np.float32(0.5) * np.cos(
        np.float32(2.0 * np.pi) * (bins.astype(np.float32) + np.float32(0.5)) / np.float32(NB)
    )
    phase = (F0 + bins)[None, :] * (np.arange(L) * LSTEP)[:, None] % S
    waves = np.cos(phase.astype(np.float32) * np.float32(2.0 * np.pi / S))
    return (taper[None, :] * waves / np.sqrt(np.float32(NSEG * NB))).astype(np.float32)


def split(value):
    high = value.astype(jnp.bfloat16)
    low = (value - high.astype(jnp.float32)).astype(jnp.bfloat16)
    return high, low


def spectra_kernel(
    lag_share,
    count_ref,
    index_ref,
    raw_ref,
    table_ref,
    weight_ref,
    out_ref,
    first_ref,
    second_ref,
    lag_ref,
    x,
    tail,
    table,
    y_even,
    y_half,
    y_odd,
    counts,
    index,
    weights,
    small_sems,
    sems,
):
    rows = x.shape[0]
    whole = S // LANES * LANES
    x_copy = pltpu.make_async_copy(raw_ref, x, sems.at[0])
    x_copy.start()
    count_copy = pltpu.make_async_copy(count_ref, counts, small_sems.at[0])
    index_copy = pltpu.make_async_copy(index_ref, index, small_sems.at[1])
    count_copy.start()
    index_copy.start()
    weight_copy = pltpu.make_async_copy(weight_ref.at[lax.axis_index("pair")], weights, small_sems.at[2])
    weight_copy.start()
    copies = []
    for g in range(CHUNKS // GROUP):
        span = pl.ds(g * GROUP * CHUNK, GROUP * CHUNK)
        copies.append(pltpu.make_async_copy(table_ref.at[span, :], table.at[span, :], sems.at[1 + g]))
        copies[-1].start()
    tail[...] = jnp.zeros_like(tail)
    x_copy.wait()
    tail[:, : S - whole] = x[:, whole:S]

    def window(start):
        base = start // LANES * LANES
        shift = start - base
        parts = []
        for lane in range(base, base + CHUNK + (LANES if shift else 0), LANES):
            if lane + LANES <= S:
                parts.append(x[:, lane : lane + LANES])
            elif lane < S:
                parts.append(tail[...])
            else:
                parts.append(jnp.zeros((rows, LANES), x.dtype))
        value = jnp.concatenate(parts, axis=1).astype(jnp.float32)
        if shift:
            value = pltpu.roll(value, value.shape[1] - shift, axis=1)[:, :CHUNK]
        return value

    even = jnp.zeros((2 * rows, 2 * LANES), jnp.float32)
    half = jnp.zeros((2 * rows, 2 * LANES), jnp.float32)
    odd = jnp.zeros((4 * rows, 4 * LANES), jnp.float32)
    for g in range(CHUNKS // GROUP):
        for c in range(g * GROUP, (g + 1) * GROUP):
            at = c * CHUNK
            x0, x1, x2, x3 = (window(m * QUARTER + at) for m in range(4))
            sum02, sum13 = x0 + x2, x1 + x3
            for target, first, value in (
                (y_even, 0, sum02 + sum13),
                (y_half, 0, sum02 - sum13),
                (y_odd, 0, x0 - x2),
                (y_odd, 2 * rows, x1 - x3),
            ):
                high, low = split(value)
                target[first : first + rows, at : at + CHUNK] = high
                target[first + rows : first + 2 * rows, at : at + CHUNK] = low
        copies[g].wait()
        lo, hi = g * GROUP * CHUNK, (g + 1) * GROUP * CHUNK
        even += jnp.dot(y_even[:, lo:hi], table[lo:hi, : 2 * LANES], preferred_element_type=jnp.float32)
        half += jnp.dot(y_half[:, lo:hi], table[lo:hi, 2 * LANES : 4 * LANES], preferred_element_type=jnp.float32)
        odd += jnp.dot(y_odd[:, lo:hi], table[lo:hi, 4 * LANES :], preferred_element_type=jnp.float32)

    even = even[:rows] + even[rows:]
    half = half[:rows] + half[rows:]
    u = odd[:rows] + odd[rows : 2 * rows]
    v = odd[2 * rows : 3 * rows] + odd[3 * rows :]
    pairs = (
        (even[:, :LANES], even[:, LANES:]),
        (half[:, :LANES], half[:, LANES:]),
        (u[:, :LANES] + v[:, LANES : 2 * LANES], u[:, LANES : 2 * LANES] - v[:, :LANES]),
        (u[:, 2 * LANES : 3 * LANES] - v[:, 3 * LANES :], u[:, 3 * LANES :] + v[:, 2 * LANES : 3 * LANES]),
    )
    power = [re * re + im * im for re, im in pairs]
    band_power = jnp.sum(power[0] + power[1] + power[2] + power[3], axis=1, keepdims=True) / NB
    pieces = []
    for (re, im), own in zip(pairs, power):
        denom = jnp.sqrt(own + water_level * band_power + 1e-06)
        pieces += [re / denom, im / denom]
    lanes = lax.broadcasted_iota(jnp.int32, (rows, LANES), 1)
    packed = []
    for p in range(7):
        moved = pltpu.roll(pieces[7], (PER - p * SPARE) % LANES, axis=1)
        packed.append(jnp.where(lanes < PER, pieces[p], moved))
    whitened = jnp.concatenate(packed, axis=1).astype(jnp.bfloat16)
    count_copy.wait()
    index_copy.wait()
    count = counts[lax.axis_index("chan")]
    source = lax.broadcasted_iota(jnp.int32, (rows, rows), 0)
    slot = lax.broadcasted_iota(jnp.int32, (rows, rows), 1)
    chosen = jnp.logical_and(source == index[...], slot < count)
    pick = jnp.where(chosen, 1.0, 0.0).astype(jnp.bfloat16)
    own = lax.dot_general(pick, whitened, (((0,), (0,)), ((), ())), preferred_element_type=jnp.float32)
    narrow = own.astype(jnp.bfloat16)
    out_ref[...] = narrow
    first_ref[...] = narrow[: rows // 2]
    second_ref[...] = narrow[rows // 2 :]
    weight_copy.wait()
    for lag in range(lag_share):
        lag_ref[lag * rows : (lag + 1) * rows, :] = (own * weights[lag : lag + 1, :]).astype(jnp.bfloat16)


def spectra(raw_rows, index_row, live_count, table, weights):
    rows = raw_rows.shape[0]
    lag_share = weights.shape[1]
    return pl.pallas_call(
        functools.partial(spectra_kernel, lag_share),
        out_shape=[
            pltpu.VMEM((rows, WIDTH), jnp.bfloat16),
            pltpu.VMEM((rows // 2, WIDTH), jnp.bfloat16),
            pltpu.VMEM((rows // 2, WIDTH), jnp.bfloat16),
            pltpu.VMEM((lag_share * rows, WIDTH), jnp.bfloat16),
        ],
        in_specs=[pl.BlockSpec(memory_space=pltpu.HBM)] * 5,
        out_specs=[pl.BlockSpec(memory_space=pltpu.VMEM)] * 4,
        scratch_shapes=[
            pltpu.VMEM((rows, S), jnp.bfloat16),
            pltpu.VMEM((rows, LANES), jnp.bfloat16),
            pltpu.VMEM((DEPTH, 8 * LANES), jnp.bfloat16),
            pltpu.VMEM((2 * rows, DEPTH), jnp.bfloat16),
            pltpu.VMEM((2 * rows, DEPTH), jnp.bfloat16),
            pltpu.VMEM((4 * rows, DEPTH), jnp.bfloat16),
            pltpu.SMEM(live_count.shape, jnp.int32),
            pltpu.VMEM(index_row.shape, jnp.int32),
            pltpu.VMEM(weights.shape[1:], jnp.float32),
            pltpu.SemaphoreType.DMA((3,)),
            pltpu.SemaphoreType.DMA((1 + CHUNKS // GROUP,)),
        ],
        compiler_params=pltpu.CompilerParams(vmem_limit_bytes=VMEM_KIB * 1024),
        cost_estimate=pl.CostEstimate(
            flops=2 * DEPTH * rows * 3072, bytes_accessed=DEPTH * 2048 + rows * S * 2, transcendentals=0
        ),
        name="spectra",
    )(*(pltpu.with_memory_space_constraint(a, pltpu.HBM) for a in (live_count, index_row, raw_rows, table, weights)))


def correlate(lag_rows, columns):
    product = lax.dot_general(
        lag_rows, columns, (((1,), (1,)), ((), ())), preferred_element_type=jnp.float32
    )
    return product.astype(jnp.bfloat16)


def eight_kernel(lags, own, side, near, far, far_swap, near_swap, cross_a, cross_b, cross_swap_a, cross_swap_b, out):
    me = lax.axis_index("chan")
    core = lax.axis_index("pair")
    x, z = me % 2, me // 2
    rows = own.shape[0]
    upper = core == 1
    lag_rows = lags[...]
    tiles = (
        ((own[...], side[...]), z),
        (
            (
                jnp.where(upper, near_swap[...], near[...]),
                jnp.where(upper, near[...], near_swap[...]),
            ),
            z ^ 1,
        ),
        ((far[...], cross_swap_a[...], cross_swap_b[...]), z ^ (2 + core)),
        ((far_swap[...], cross_a[...], cross_b[...]), z ^ (3 - core)),
    )
    for blocks, plane in tiles:
        columns = jnp.concatenate(blocks, axis=0)
        product = lax.dot_general(
            lag_rows, columns, (((1,), (1,)), ((), ())), preferred_element_type=jnp.float32
        )
        product = jnp.where(x == 0, product, pltpu.roll(product, rows, axis=1)).astype(jnp.bfloat16)
        at = pl.multiple_of(plane * 2 * rows, 2 * rows)
        for lag in range(out.shape[0]):
            out[lag, :, pl.ds(at, 2 * rows)] = product[lag * rows : (lag + 1) * rows]


def exchange_eight(own, first, second, lags):
    def split_move(mask1, mask0):
        pairs = [(2 * c + 1, 2 * (c ^ mask1) + 1) for c in range(8)] + [(2 * c, 2 * (c ^ mask0)) for c in range(8)]
        return lambda a: lax.ppermute(a, ("chan", "pair"), pairs)

    def forward(a):
        pairs = [(2 * c + p, 2 * (c ^ 1) + 1 - p) for c in range(8) for p in range(2)]
        return lax.ppermute(a, ("chan", "pair"), pairs)

    def swap(a):
        return lax.ppermute(a, "pair", [(0, 1), (1, 0)])

    far_a = split_move(6, 4)(first)
    far_b = split_move(6, 4)(second)
    side = split_move(1, 1)(own)
    near = split_move(3, 2)(own)
    q, near = lax.optimization_barrier((far_a, near))
    cross_a = forward(q)
    _, cross_a = lax.optimization_barrier((far_b, cross_a))
    cross_b = forward(far_b)
    far = jnp.concatenate([far_a, far_b], axis=0)
    far_swap, near_swap = swap(far), swap(near)
    cross_swap_a, cross_swap_b = swap(cross_a), swap(cross_b)
    lag_share, rows = lags.shape[0] // own.shape[0], own.shape[0]
    return pl.pallas_call(
        eight_kernel,
        out_shape=jax.ShapeDtypeStruct((lag_share, rows, 8 * rows), jnp.bfloat16),
        in_specs=[pl.BlockSpec(memory_space=pltpu.VMEM)] * 11,
        out_specs=pl.BlockSpec(memory_space=pltpu.VMEM),
        compiler_params=pltpu.CompilerParams(vmem_limit_bytes=CORR_KIB * 1024),
        cost_estimate=pl.CostEstimate(
            flops=2 * lag_share * rows * 8 * rows * WIDTH, bytes_accessed=12 * rows * WIDTH * 2, transcendentals=0
        ),
        name="correlate",
    )(lags, own, side, near, far, far_swap, near_swap, cross_a, cross_b, cross_swap_a, cross_swap_b)


def shards(table, weights, raw, live_index, live_count):
    slot_count, seg_count, samples = raw.shape
    pairs = lax.axis_size("pair")
    own, first, second, lags = spectra(
        raw.reshape(slot_count * seg_count, samples),
        live_index,
        live_count,
        table,
        weights.reshape(pairs, L // pairs, WIDTH),
    )
    if lax.axis_size("chan") == 8 and pairs == 2 and slot_count == 64:
        return exchange_eight(own, first, second, lags)
    product = correlate(lags, lax.all_gather(own, "chan", axis=0, tiled=True))
    return product.reshape(L // pairs, slot_count, -1)


def solution(mesh):
    local = functools.partial(shards, jnp.asarray(quarter_table()), jnp.asarray(lag_table()))
    return jax.shard_map(
        local,
        mesh=mesh,
        in_specs=(P(("groups", "chan"), None, None), P(("groups", "chan"), None), P("groups")),
        out_specs=P("pair", ("groups", "chan"), None),
        check_vma=False,
    )
```

```python
import functools

import jax
import jax.numpy as jnp
import numpy as np
from jax import lax
from jax.experimental import pallas as pl
from jax.experimental.pallas import tpu as pltpu
from jax.sharding import PartitionSpec as P

S = 12000
NB = 448
NSEG = 1
L = 6
LSTEP = 125
F0 = 60

water_level = 0.1

QUARTER = S // 4
CHUNK = 256
CHUNKS = -(-QUARTER // CHUNK)
DEPTH = CHUNKS * CHUNK
GROUPS = (2, 2, 2, 2, 2, 2)
RES = (0, 2, 1, 3)
PER = NB // 4
LANES = 128
SPARE = LANES - PER
WIDTH = 2 * NB
VMEM_KIB = 40 * 1024
CORR_KIB = 32 * 1024


def bins_of(residue):
    return np.arange(residue, NB, 4)


def quarter_table():
    table = np.zeros((DEPTH, 8 * LANES), np.float64)
    t = np.arange(QUARTER, dtype=np.int64)
    step = np.float64(np.float32(2.0 * np.pi / S))
    for place, residue in enumerate(RES):
        angles = (t[:, None] * (F0 + bins_of(residue))[None, :] % S) * step
        at = 2 * place * LANES
        table[:QUARTER, at : at + PER] = np.cos(angles)
        table[:QUARTER, at + LANES : at + LANES + PER] = -np.sin(angles)
    return table.astype(np.float32).astype(jnp.bfloat16)


def packed_bins():
    pieces = [bins_of(residue) for residue in RES for _ in range(2)]
    columns = []
    for p in range(7):
        columns.append(pieces[p])
        columns.append(pieces[7][p * SPARE : (p + 1) * SPARE])
    return np.concatenate(columns)


def lag_table():
    bins = packed_bins()
    taper = np.float32(0.5) - np.float32(0.5) * np.cos(
        np.float32(2.0 * np.pi) * (bins.astype(np.float32) + np.float32(0.5)) / np.float32(NB)
    )
    phase = (F0 + bins)[None, :] * (np.arange(L) * LSTEP)[:, None] % S
    waves = np.cos(phase.astype(np.float32) * np.float32(2.0 * np.pi / S))
    return (taper[None, :] * waves / np.sqrt(np.float32(NSEG * NB))).astype(np.float32)


def split(value):
    high = value.astype(jnp.bfloat16)
    low = (value - high.astype(jnp.float32)).astype(jnp.bfloat16)
    return high, low


def spectra_kernel(
    lag_share,
    count_ref,
    index_ref,
    raw_ref,
    table_ref,
    weight_ref,
    out_ref,
    first_ref,
    second_ref,
    lag_ref,
    x,
    tail,
    table,
    y_even,
    y_half,
    y_odd,
    counts,
    index,
    weights,
    small_sems,
    sems,
):
    rows = x.shape[0]
    whole = S // LANES * LANES
    x_copy = pltpu.make_async_copy(raw_ref, x, sems.at[0])
    x_copy.start()
    count_copy = pltpu.make_async_copy(count_ref, counts, small_sems.at[0])
    index_copy = pltpu.make_async_copy(index_ref, index, small_sems.at[1])
    count_copy.start()
    index_copy.start()
    weight_copy = pltpu.make_async_copy(weight_ref.at[lax.axis_index("pair")], weights, small_sems.at[2])
    weight_copy.start()
    copies = []
    ends = np.cumsum(GROUPS)
    for g, end in enumerate(ends):
        span = pl.ds(int(end - GROUPS[g]) * CHUNK, GROUPS[g] * CHUNK)
        copies.append(pltpu.make_async_copy(table_ref.at[span, :], table.at[span, :], sems.at[1 + g]))
        copies[-1].start()
    tail[...] = jnp.zeros_like(tail)
    x_copy.wait()
    tail[:, : S - whole] = x[:, whole:S]

    def window(start):
        base = start // LANES * LANES
        shift = start - base
        parts = []
        for lane in range(base, base + CHUNK + (LANES if shift else 0), LANES):
            if lane + LANES <= S:
                parts.append(x[:, lane : lane + LANES])
            elif lane < S:
                parts.append(tail[...])
            else:
                parts.append(jnp.zeros((rows, LANES), x.dtype))
        value = jnp.concatenate(parts, axis=1).astype(jnp.float32)
        if shift:
            value = pltpu.roll(value, value.shape[1] - shift, axis=1)[:, :CHUNK]
        return value

    even = jnp.zeros((2 * rows, 2 * LANES), jnp.float32)
    half = jnp.zeros((2 * rows, 2 * LANES), jnp.float32)
    odd = jnp.zeros((4 * rows, 4 * LANES), jnp.float32)
    for g, end in enumerate(ends):
        for c in range(int(end) - GROUPS[g], int(end)):
            at = c * CHUNK
            x0, x1, x2, x3 = (window(m * QUARTER + at) for m in range(4))
            sum02, sum13 = x0 + x2, x1 + x3
            for target, first, value in (
                (y_even, 0, sum02 + sum13),
                (y_half, 0, sum02 - sum13),
                (y_odd, 0, x0 - x2),
                (y_odd, 2 * rows, x1 - x3),
            ):
                high, low = split(value)
                target[first : first + rows, at : at + CHUNK] = high
                target[first + rows : first + 2 * rows, at : at + CHUNK] = low
        copies[g].wait()
        lo, hi = int(end - GROUPS[g]) * CHUNK, int(end) * CHUNK
        even += jnp.dot(y_even[:, lo:hi], table[lo:hi, : 2 * LANES], preferred_element_type=jnp.float32)
        half += jnp.dot(y_half[:, lo:hi], table[lo:hi, 2 * LANES : 4 * LANES], preferred_element_type=jnp.float32)
        odd += jnp.dot(y_odd[:, lo:hi], table[lo:hi, 4 * LANES :], preferred_element_type=jnp.float32)

    even = even[:rows] + even[rows:]
    half = half[:rows] + half[rows:]
    u = odd[:rows] + odd[rows : 2 * rows]
    v = odd[2 * rows : 3 * rows] + odd[3 * rows :]
    pairs = (
        (even[:, :LANES], even[:, LANES:]),
        (half[:, :LANES], half[:, LANES:]),
        (u[:, :LANES] + v[:, LANES : 2 * LANES], u[:, LANES : 2 * LANES] - v[:, :LANES]),
        (u[:, 2 * LANES : 3 * LANES] - v[:, 3 * LANES :], u[:, 3 * LANES :] + v[:, 2 * LANES : 3 * LANES]),
    )
    power = [re * re + im * im for re, im in pairs]
    band_power = jnp.sum(power[0] + power[1] + power[2] + power[3], axis=1, keepdims=True) / NB
    pieces = []
    for (re, im), own in zip(pairs, power):
        denom = jnp.sqrt(own + water_level * band_power + 1e-06)
        pieces += [re / denom, im / denom]
    lanes = lax.broadcasted_iota(jnp.int32, (rows, LANES), 1)
    packed = []
    for p in range(7):
        moved = pltpu.roll(pieces[7], (PER - p * SPARE) % LANES, axis=1)
        packed.append(jnp.where(lanes < PER, pieces[p], moved))
    whitened = jnp.concatenate(packed, axis=1).astype(jnp.bfloat16)
    count_copy.wait()
    index_copy.wait()
    count = counts[lax.axis_index("chan")]
    source = lax.broadcasted_iota(jnp.int32, (rows, rows), 0)
    slot = lax.broadcasted_iota(jnp.int32, (rows, rows), 1)
    chosen = jnp.logical_and(source == index[...], slot < count)
    pick = jnp.where(chosen, 1.0, 0.0).astype(jnp.bfloat16)
    own = lax.dot_general(pick, whitened, (((0,), (0,)), ((), ())), preferred_element_type=jnp.float32)
    narrow = own.astype(jnp.bfloat16)
    out_ref[...] = narrow
    first_ref[...] = narrow[: rows // 2]
    second_ref[...] = narrow[rows // 2 :]
    weight_copy.wait()
    for lag in range(lag_share):
        lag_ref[lag * rows : (lag + 1) * rows, :] = (own * weights[lag : lag + 1, :]).astype(jnp.bfloat16)


def spectra(raw_rows, index_row, live_count, table, weights):
    rows = raw_rows.shape[0]
    lag_share = weights.shape[1]
    return pl.pallas_call(
        functools.partial(spectra_kernel, lag_share),
        out_shape=[
            pltpu.VMEM((rows, WIDTH), jnp.bfloat16),
            pltpu.VMEM((rows // 2, WIDTH), jnp.bfloat16),
            pltpu.VMEM((rows // 2, WIDTH), jnp.bfloat16),
            pltpu.VMEM((lag_share * rows, WIDTH), jnp.bfloat16),
        ],
        in_specs=[pl.BlockSpec(memory_space=pltpu.HBM)] * 5,
        out_specs=[pl.BlockSpec(memory_space=pltpu.VMEM)] * 4,
        scratch_shapes=[
            pltpu.VMEM((rows, S), jnp.bfloat16),
            pltpu.VMEM((rows, LANES), jnp.bfloat16),
            pltpu.VMEM((DEPTH, 8 * LANES), jnp.bfloat16),
            pltpu.VMEM((2 * rows, DEPTH), jnp.bfloat16),
            pltpu.VMEM((2 * rows, DEPTH), jnp.bfloat16),
            pltpu.VMEM((4 * rows, DEPTH), jnp.bfloat16),
            pltpu.SMEM(live_count.shape, jnp.int32),
            pltpu.VMEM(index_row.shape, jnp.int32),
            pltpu.VMEM(weights.shape[1:], jnp.float32),
            pltpu.SemaphoreType.DMA((3,)),
            pltpu.SemaphoreType.DMA((1 + len(GROUPS),)),
        ],
        compiler_params=pltpu.CompilerParams(vmem_limit_bytes=VMEM_KIB * 1024),
        cost_estimate=pl.CostEstimate(
            flops=2 * DEPTH * rows * 3072, bytes_accessed=DEPTH * 2048 + rows * S * 2, transcendentals=0
        ),
        name="spectra",
    )(*(pltpu.with_memory_space_constraint(a, pltpu.HBM) for a in (live_count, index_row, raw_rows, table, weights)))


def correlate(lag_rows, columns):
    product = lax.dot_general(
        lag_rows, columns, (((1,), (1,)), ((), ())), preferred_element_type=jnp.float32
    )
    return product.astype(jnp.bfloat16)


def eight_kernel(lags, own, side, near, far, far_swap, near_swap, cross_a, cross_b, cross_swap_a, cross_swap_b, out):
    me = lax.axis_index("chan")
    core = lax.axis_index("pair")
    x, z = me % 2, me // 2
    rows = own.shape[0]
    upper = core == 1
    lag_rows = lags[...]
    tiles = (
        ((own[...], side[...]), z),
        (
            (
                jnp.where(upper, near_swap[...], near[...]),
                jnp.where(upper, near[...], near_swap[...]),
            ),
            z ^ 1,
        ),
        ((far[...], cross_swap_a[...], cross_swap_b[...]), z ^ (2 + core)),
        ((far_swap[...], cross_a[...], cross_b[...]), z ^ (3 - core)),
    )
    for blocks, plane in tiles:
        columns = jnp.concatenate(blocks, axis=0)
        product = lax.dot_general(
            lag_rows, columns, (((1,), (1,)), ((), ())), preferred_element_type=jnp.float32
        )
        product = jnp.where(x == 0, product, pltpu.roll(product, rows, axis=1)).astype(jnp.bfloat16)
        at = pl.multiple_of(plane * 2 * rows, 2 * rows)
        for lag in range(out.shape[0]):
            out[lag, :, pl.ds(at, 2 * rows)] = product[lag * rows : (lag + 1) * rows]


def exchange_eight(own, first, second, lags):
    def split_move(mask1, mask0):
        pairs = [(2 * c + 1, 2 * (c ^ mask1) + 1) for c in range(8)] + [(2 * c, 2 * (c ^ mask0)) for c in range(8)]
        return lambda a: lax.ppermute(a, ("chan", "pair"), pairs)

    def forward(a):
        pairs = [(2 * c + p, 2 * (c ^ 1) + 1 - p) for c in range(8) for p in range(2)]
        return lax.ppermute(a, ("chan", "pair"), pairs)

    def swap(a):
        return lax.ppermute(a, "pair", [(0, 1), (1, 0)])

    far_a = split_move(6, 4)(first)
    far_b = split_move(6, 4)(second)
    side = split_move(1, 1)(own)
    near = split_move(3, 2)(own)
    cross_a = forward(far_a)
    cross_b = forward(far_b)
    cross_a, near, side = lax.optimization_barrier((cross_a, near, side))
    cross_swap_a = swap(cross_a)
    cross_b, cross_swap_a = lax.optimization_barrier((cross_b, cross_swap_a))
    far = jnp.concatenate([far_a, far_b], axis=0)
    far_swap = swap(far)
    near_swap = swap(near)
    cross_swap_b = swap(cross_b)
    lag_share, rows = lags.shape[0] // own.shape[0], own.shape[0]
    return pl.pallas_call(
        eight_kernel,
        out_shape=jax.ShapeDtypeStruct((lag_share, rows, 8 * rows), jnp.bfloat16),
        in_specs=[pl.BlockSpec(memory_space=pltpu.VMEM)] * 11,
        out_specs=pl.BlockSpec(memory_space=pltpu.VMEM),
        compiler_params=pltpu.CompilerParams(vmem_limit_bytes=CORR_KIB * 1024),
        cost_estimate=pl.CostEstimate(
            flops=2 * lag_share * rows * 8 * rows * WIDTH, bytes_accessed=12 * rows * WIDTH * 2, transcendentals=0
        ),
        name="correlate",
    )(lags, own, side, near, far, far_swap, near_swap, cross_a, cross_b, cross_swap_a, cross_swap_b)


def shards(table, weights, raw, live_index, live_count):
    slot_count, seg_count, samples = raw.shape
    pairs = lax.axis_size("pair")
    own, first, second, lags = spectra(
        raw.reshape(slot_count * seg_count, samples),
        live_index,
        live_count,
        table,
        weights.reshape(pairs, L // pairs, WIDTH),
    )
    if lax.axis_size("chan") == 8 and pairs == 2 and slot_count == 64:
        return exchange_eight(own, first, second, lags)
    product = correlate(lags, lax.all_gather(own, "chan", axis=0, tiled=True))
    return product.reshape(L // pairs, slot_count, -1)


def solution(mesh):
    local = functools.partial(shards, jnp.asarray(quarter_table()), jnp.asarray(lag_table()))
    return jax.shard_map(
        local,
        mesh=mesh,
        in_specs=(P(("groups", "chan"), None, None), P(("groups", "chan"), None), P("groups")),
        out_specs=P("pair", ("groups", "chan"), None),
        check_vma=False,
    )
```

```python
import functools

import jax
import jax.numpy as jnp
import numpy as np
from jax import lax
from jax.experimental import pallas as pl
from jax.experimental.pallas import tpu as pltpu
from jax.sharding import PartitionSpec as P

S = 12000
NB = 448
NSEG = 1
L = 6
LSTEP = 125
F0 = 60

water_level = 0.1

QUARTER = S // 4
CHUNK = 256
CHUNKS = -(-QUARTER // CHUNK)
DEPTH = CHUNKS * CHUNK
GROUPS = (2, 2, 2, 2, 2, 2)
RES = (0, 2, 1, 3)
PER = NB // 4
LANES = 128
SPARE = LANES - PER
WIDTH = 2 * NB
VMEM_KIB = 40 * 1024
CORR_KIB = 32 * 1024


def bins_of(residue):
    return np.arange(residue, NB, 4)


def quarter_table():
    table = np.zeros((DEPTH, 8 * LANES), np.float64)
    t = np.arange(QUARTER, dtype=np.int64)
    step = np.float64(np.float32(2.0 * np.pi / S))
    for place, residue in enumerate(RES):
        angles = (t[:, None] * (F0 + bins_of(residue))[None, :] % S) * step
        at = 2 * place * LANES
        table[:QUARTER, at : at + PER] = np.cos(angles)
        table[:QUARTER, at + LANES : at + LANES + PER] = -np.sin(angles)
    return table.astype(np.float32).astype(jnp.bfloat16)


def packed_bins():
    pieces = [bins_of(residue) for residue in RES for _ in range(2)]
    columns = []
    for p in range(7):
        columns.append(pieces[p])
        columns.append(pieces[7][p * SPARE : (p + 1) * SPARE])
    return np.concatenate(columns)


def lag_table():
    bins = packed_bins()
    taper = np.float32(0.5) - np.float32(0.5) * np.cos(
        np.float32(2.0 * np.pi) * (bins.astype(np.float32) + np.float32(0.5)) / np.float32(NB)
    )
    phase = (F0 + bins)[None, :] * (np.arange(L) * LSTEP)[:, None] % S
    waves = np.cos(phase.astype(np.float32) * np.float32(2.0 * np.pi / S))
    return (taper[None, :] * waves / np.sqrt(np.float32(NSEG * NB))).astype(np.float32)


def split(value):
    high = value.astype(jnp.bfloat16)
    low = (value - high.astype(jnp.float32)).astype(jnp.bfloat16)
    return high, low


def spectra_kernel(
    lag_share,
    count_ref,
    index_ref,
    raw_ref,
    table_ref,
    weight_ref,
    out_ref,
    first_ref,
    second_ref,
    lag_ref,
    x,
    tail,
    table,
    y_even,
    y_half,
    y_odd,
    counts,
    index,
    weights,
    small_sems,
    sems,
):
    rows = x.shape[0]
    whole = S // LANES * LANES
    x_copy = pltpu.make_async_copy(raw_ref, x, sems.at[0])
    x_copy.start()
    count_copy = pltpu.make_async_copy(count_ref, counts, small_sems.at[0])
    index_copy = pltpu.make_async_copy(index_ref, index, small_sems.at[1])
    count_copy.start()
    index_copy.start()
    weight_copy = pltpu.make_async_copy(weight_ref.at[lax.axis_index("pair")], weights, small_sems.at[2])
    weight_copy.start()
    copies = []
    ends = np.cumsum(GROUPS)
    for g, end in enumerate(ends):
        span = pl.ds(int(end - GROUPS[g]) * CHUNK, GROUPS[g] * CHUNK)
        copies.append(pltpu.make_async_copy(table_ref.at[span, :], table.at[span, :], sems.at[1 + g]))
        copies[-1].start()
    tail[...] = jnp.zeros_like(tail)
    x_copy.wait()
    tail[:, : S - whole] = x[:, whole:S]

    def window(start):
        base = start // LANES * LANES
        shift = start - base
        parts = []
        for lane in range(base, base + CHUNK + (LANES if shift else 0), LANES):
            if lane + LANES <= S:
                parts.append(x[:, lane : lane + LANES])
            elif lane < S:
                parts.append(tail[...])
            else:
                parts.append(jnp.zeros((rows, LANES), x.dtype))
        value = jnp.concatenate(parts, axis=1).astype(jnp.float32)
        if shift:
            value = pltpu.roll(value, value.shape[1] - shift, axis=1)[:, :CHUNK]
        return value

    even = jnp.zeros((2 * rows, 2 * LANES), jnp.float32)
    half = jnp.zeros((2 * rows, 2 * LANES), jnp.float32)
    odd = jnp.zeros((4 * rows, 4 * LANES), jnp.float32)
    for g, end in enumerate(ends):
        for c in range(int(end) - GROUPS[g], int(end)):
            at = c * CHUNK
            x0, x1, x2, x3 = (window(m * QUARTER + at) for m in range(4))
            sum02, sum13 = x0 + x2, x1 + x3
            for target, first, value in (
                (y_even, 0, sum02 + sum13),
                (y_half, 0, sum02 - sum13),
                (y_odd, 0, x0 - x2),
                (y_odd, 2 * rows, x1 - x3),
            ):
                high, low = split(value)
                target[first : first + rows, at : at + CHUNK] = high
                target[first + rows : first + 2 * rows, at : at + CHUNK] = low
        copies[g].wait()
        lo, hi = int(end - GROUPS[g]) * CHUNK, int(end) * CHUNK
        even += jnp.dot(y_even[:, lo:hi], table[lo:hi, : 2 * LANES], preferred_element_type=jnp.float32)
        half += jnp.dot(y_half[:, lo:hi], table[lo:hi, 2 * LANES : 4 * LANES], preferred_element_type=jnp.float32)
        odd += jnp.dot(y_odd[:, lo:hi], table[lo:hi, 4 * LANES :], preferred_element_type=jnp.float32)

    even = even[:rows] + even[rows:]
    half = half[:rows] + half[rows:]
    u = odd[:rows] + odd[rows : 2 * rows]
    v = odd[2 * rows : 3 * rows] + odd[3 * rows :]
    pairs = (
        (even[:, :LANES], even[:, LANES:]),
        (half[:, :LANES], half[:, LANES:]),
        (u[:, :LANES] + v[:, LANES : 2 * LANES], u[:, LANES : 2 * LANES] - v[:, :LANES]),
        (u[:, 2 * LANES : 3 * LANES] - v[:, 3 * LANES :], u[:, 3 * LANES :] + v[:, 2 * LANES : 3 * LANES]),
    )
    power = [re * re + im * im for re, im in pairs]
    band_power = jnp.sum(power[0] + power[1] + power[2] + power[3], axis=1, keepdims=True) / NB
    pieces = []
    for (re, im), own in zip(pairs, power):
        scale = 1.0 / jnp.sqrt(own + water_level * band_power + 1e-06)
        pieces += [re * scale, im * scale]
    lanes = lax.broadcasted_iota(jnp.int32, (rows, LANES), 1)
    packed = []
    for p in range(7):
        moved = pltpu.roll(pieces[7], (PER - p * SPARE) % LANES, axis=1)
        packed.append(jnp.where(lanes < PER, pieces[p], moved))
    whitened = jnp.concatenate(packed, axis=1).astype(jnp.bfloat16)
    count_copy.wait()
    index_copy.wait()
    count = counts[lax.axis_index("chan")]
    source = lax.broadcasted_iota(jnp.int32, (rows, rows), 0)
    slot = lax.broadcasted_iota(jnp.int32, (rows, rows), 1)
    chosen = jnp.logical_and(source == index[...], slot < count)
    pick = jnp.where(chosen, 1.0, 0.0).astype(jnp.bfloat16)
    own = lax.dot_general(pick, whitened, (((0,), (0,)), ((), ())), preferred_element_type=jnp.float32)
    narrow = own.astype(jnp.bfloat16)
    out_ref[...] = narrow
    first_ref[...] = narrow[: rows // 2]
    second_ref[...] = narrow[rows // 2 :]
    weight_copy.wait()
    for lag in range(lag_share):
        lag_ref[lag * rows : (lag + 1) * rows, :] = (own * weights[lag : lag + 1, :]).astype(jnp.bfloat16)


def spectra(raw_rows, index_row, live_count, table, weights):
    rows = raw_rows.shape[0]
    lag_share = weights.shape[1]
    return pl.pallas_call(
        functools.partial(spectra_kernel, lag_share),
        out_shape=[
            pltpu.VMEM((rows, WIDTH), jnp.bfloat16),
            pltpu.VMEM((rows // 2, WIDTH), jnp.bfloat16),
            pltpu.VMEM((rows // 2, WIDTH), jnp.bfloat16),
            pltpu.VMEM((lag_share * rows, WIDTH), jnp.bfloat16),
        ],
        in_specs=[pl.BlockSpec(memory_space=pltpu.HBM)] * 5,
        out_specs=[pl.BlockSpec(memory_space=pltpu.VMEM)] * 4,
        scratch_shapes=[
            pltpu.VMEM((rows, S), jnp.bfloat16),
            pltpu.VMEM((rows, LANES), jnp.bfloat16),
            pltpu.VMEM((DEPTH, 8 * LANES), jnp.bfloat16),
            pltpu.VMEM((2 * rows, DEPTH), jnp.bfloat16),
            pltpu.VMEM((2 * rows, DEPTH), jnp.bfloat16),
            pltpu.VMEM((4 * rows, DEPTH), jnp.bfloat16),
            pltpu.SMEM(live_count.shape, jnp.int32),
            pltpu.VMEM(index_row.shape, jnp.int32),
            pltpu.VMEM(weights.shape[1:], jnp.float32),
            pltpu.SemaphoreType.DMA((3,)),
            pltpu.SemaphoreType.DMA((1 + len(GROUPS),)),
        ],
        compiler_params=pltpu.CompilerParams(vmem_limit_bytes=VMEM_KIB * 1024),
        cost_estimate=pl.CostEstimate(
            flops=2 * DEPTH * rows * 3072, bytes_accessed=DEPTH * 2048 + rows * S * 2, transcendentals=0
        ),
        name="spectra",
    )(*(pltpu.with_memory_space_constraint(a, pltpu.HBM) for a in (live_count, index_row, raw_rows, table, weights)))


def correlate(lag_rows, columns):
    product = lax.dot_general(
        lag_rows, columns, (((1,), (1,)), ((), ())), preferred_element_type=jnp.float32
    )
    return product.astype(jnp.bfloat16)


def put(out, product, plane, rows):
    at = pl.multiple_of(plane * 2 * rows, 2 * rows)
    for lag in range(out.shape[0]):
        out[lag, :, pl.ds(at, 2 * rows)] = product[lag * rows : (lag + 1) * rows]


def plane_products(lag_rows, tiles, x, rows):
    columns = jnp.concatenate([block for blocks in tiles for block in blocks], axis=0)
    both = lax.dot_general(lag_rows, columns, (((1,), (1,)), ((), ())), preferred_element_type=jnp.float32)
    products = [both[:, place * 2 * rows : (place + 1) * 2 * rows] for place in range(len(tiles))]
    return [jnp.where(x == 0, p, pltpu.roll(p, rows, axis=1)).astype(jnp.bfloat16) for p in products]


def early_kernel(lags, own, side, near, near_swap, out):
    x = lax.axis_index("chan") % 2
    upper = lax.axis_index("pair") == 1
    nearest = (
        jnp.where(upper, near_swap[...], near[...]),
        jnp.where(upper, near[...], near_swap[...]),
    )
    tiles = ((own[...], side[...]), nearest)
    for place, product in enumerate(plane_products(lags[...], tiles, x, own.shape[0])):
        out[place] = product


def late_kernel(lags, early, far, far_swap, cross_a, cross_b, cross_swap_a, cross_swap_b, out):
    me = lax.axis_index("chan")
    core = lax.axis_index("pair")
    x, z = me % 2, me // 2
    rows = far.shape[0]
    tiles = (
        (far[...], cross_swap_a[...], cross_swap_b[...]),
        (far_swap[...], cross_a[...], cross_b[...]),
    )
    put(out, early[0], z, rows)
    put(out, early[1], z ^ 1, rows)
    first, second = plane_products(lags[...], tiles, x, rows)
    put(out, first, z ^ (2 + core), rows)
    put(out, second, z ^ (3 - core), rows)


def exchange_eight(own, first, second, lags):
    def split_move(mask1, mask0):
        pairs = [(2 * c + 1, 2 * (c ^ mask1) + 1) for c in range(8)] + [(2 * c, 2 * (c ^ mask0)) for c in range(8)]
        return lambda a: lax.ppermute(a, ("chan", "pair"), pairs)

    def forward(a):
        pairs = [(2 * c + p, 2 * (c ^ 1) + 1 - p) for c in range(8) for p in range(2)]
        return lax.ppermute(a, ("chan", "pair"), pairs)

    def swap(a):
        return lax.ppermute(a, "pair", [(0, 1), (1, 0)])

    far_a = split_move(6, 4)(first)
    far_b = split_move(6, 4)(second)
    side = split_move(1, 1)(own)
    near = split_move(3, 2)(own)
    cross_a = forward(far_a)
    cross_b = forward(far_b)
    cross_a, near, side = lax.optimization_barrier((cross_a, near, side))
    cross_swap_a = swap(cross_a)
    cross_b, cross_swap_a = lax.optimization_barrier((cross_b, cross_swap_a))
    far = jnp.concatenate([far_a, far_b], axis=0)
    far_swap = swap(far)
    near_swap = swap(near)
    cross_swap_b = swap(cross_b)
    lag_share, rows = lags.shape[0] // own.shape[0], own.shape[0]
    early = pl.pallas_call(
        early_kernel,
        out_shape=pltpu.VMEM((2, lag_share * rows, 2 * rows), jnp.bfloat16),
        in_specs=[pl.BlockSpec(memory_space=pltpu.VMEM)] * 5,
        out_specs=pl.BlockSpec(memory_space=pltpu.VMEM),
        compiler_params=pltpu.CompilerParams(vmem_limit_bytes=CORR_KIB * 1024),
        cost_estimate=pl.CostEstimate(
            flops=2 * lag_share * rows * 4 * rows * WIDTH, bytes_accessed=8 * rows * WIDTH * 2, transcendentals=0
        ),
        name="correlate_early",
    )(lags, own, side, near, near_swap)
    return pl.pallas_call(
        late_kernel,
        out_shape=jax.ShapeDtypeStruct((lag_share, rows, 8 * rows), jnp.bfloat16),
        in_specs=[pl.BlockSpec(memory_space=pltpu.VMEM)] * 8,
        out_specs=pl.BlockSpec(memory_space=pltpu.VMEM),
        compiler_params=pltpu.CompilerParams(vmem_limit_bytes=CORR_KIB * 1024),
        cost_estimate=pl.CostEstimate(
            flops=2 * lag_share * rows * 4 * rows * WIDTH, bytes_accessed=8 * rows * WIDTH * 2, transcendentals=0
        ),
        name="correlate_late",
    )(lags, early, far, far_swap, cross_a, cross_b, cross_swap_a, cross_swap_b)


def shards(table, weights, raw, live_index, live_count):
    slot_count, seg_count, samples = raw.shape
    pairs = lax.axis_size("pair")
    own, first, second, lags = spectra(
        raw.reshape(slot_count * seg_count, samples),
        live_index,
        live_count,
        table,
        weights.reshape(pairs, L // pairs, WIDTH),
    )
    if lax.axis_size("chan") == 8 and pairs == 2 and slot_count == 64:
        return exchange_eight(own, first, second, lags)
    product = correlate(lags, lax.all_gather(own, "chan", axis=0, tiled=True))
    return product.reshape(L // pairs, slot_count, -1)


def solution(mesh):
    local = functools.partial(shards, jnp.asarray(quarter_table()), jnp.asarray(lag_table()))
    return jax.shard_map(
        local,
        mesh=mesh,
        in_specs=(P(("groups", "chan"), None, None), P(("groups", "chan"), None), P("groups")),
        out_specs=P("pair", ("groups", "chan"), None),
        check_vma=False,
    )
```

```python
import functools

import jax
import jax.numpy as jnp
import numpy as np
from jax import lax
from jax.experimental import pallas as pl
from jax.experimental.pallas import tpu as pltpu
from jax.sharding import PartitionSpec as P

S = 12000
NB = 448
NSEG = 1
L = 6
LSTEP = 125
F0 = 60

water_level = 0.1

QUARTER = S // 4
CHUNK = 256
CHUNKS = -(-QUARTER // CHUNK)
DEPTH = CHUNKS * CHUNK
GROUPS = (2, 2, 2, 2, 2, 2)
RES = (0, 2, 1, 3)
PER = NB // 4
LANES = 128
SPARE = LANES - PER
WIDTH = 2 * NB
VMEM_KIB = 40 * 1024
CORR_KIB = 32 * 1024


def bins_of(residue):
    return np.arange(residue, NB, 4)


def quarter_table():
    table = np.zeros((DEPTH, 8 * LANES), np.float64)
    t = np.arange(QUARTER, dtype=np.int64)
    step = np.float64(np.float32(2.0 * np.pi / S))
    for place, residue in enumerate(RES):
        angles = (t[:, None] * (F0 + bins_of(residue))[None, :] % S) * step
        at = 2 * place * LANES
        table[:QUARTER, at : at + PER] = np.cos(angles)
        table[:QUARTER, at + LANES : at + LANES + PER] = -np.sin(angles)
    return table.astype(np.float32).astype(jnp.bfloat16)


def packed_bins():
    pieces = [bins_of(residue) for residue in RES for _ in range(2)]
    columns = []
    for p in range(7):
        columns.append(pieces[p])
        columns.append(pieces[7][p * SPARE : (p + 1) * SPARE])
    return np.concatenate(columns)


def lag_table():
    bins = packed_bins()
    taper = np.float32(0.5) - np.float32(0.5) * np.cos(
        np.float32(2.0 * np.pi) * (bins.astype(np.float32) + np.float32(0.5)) / np.float32(NB)
    )
    phase = (F0 + bins)[None, :] * (np.arange(L) * LSTEP)[:, None] % S
    waves = np.cos(phase.astype(np.float32) * np.float32(2.0 * np.pi / S))
    return (taper[None, :] * waves / np.sqrt(np.float32(NSEG * NB))).astype(np.float32)


def split(value):
    high = value.astype(jnp.bfloat16)
    low = (value - high.astype(jnp.float32)).astype(jnp.bfloat16)
    return high, low


def spectra_kernel(
    lag_share,
    count_ref,
    index_ref,
    raw_ref,
    table_ref,
    weight_ref,
    out_ref,
    first_ref,
    second_ref,
    lag_ref,
    x,
    tail,
    table,
    y_even,
    y_half,
    y_odd,
    counts,
    index,
    weights,
    small_sems,
    sems,
):
    rows = x.shape[0]
    whole = S // LANES * LANES
    x_copy = pltpu.make_async_copy(raw_ref, x, sems.at[0])
    x_copy.start()
    count_copy = pltpu.make_async_copy(count_ref, counts, small_sems.at[0])
    index_copy = pltpu.make_async_copy(index_ref, index, small_sems.at[1])
    count_copy.start()
    index_copy.start()
    weight_copy = pltpu.make_async_copy(weight_ref.at[lax.axis_index("pair")], weights, small_sems.at[2])
    weight_copy.start()
    copies = []
    ends = np.cumsum(GROUPS)
    for g, end in enumerate(ends):
        span = pl.ds(int(end - GROUPS[g]) * CHUNK, GROUPS[g] * CHUNK)
        copies.append(pltpu.make_async_copy(table_ref.at[span, :], table.at[span, :], sems.at[1 + g]))
        copies[-1].start()
    tail[...] = jnp.zeros_like(tail)
    x_copy.wait()
    tail[:, : S - whole] = x[:, whole:S]

    def window(start):
        base = start // LANES * LANES
        shift = start - base
        parts = []
        for lane in range(base, base + CHUNK + (LANES if shift else 0), LANES):
            if lane + LANES <= S:
                parts.append(x[:, lane : lane + LANES])
            elif lane < S:
                parts.append(tail[...])
            else:
                parts.append(jnp.zeros((rows, LANES), x.dtype))
        value = jnp.concatenate(parts, axis=1).astype(jnp.float32)
        if shift:
            value = pltpu.roll(value, value.shape[1] - shift, axis=1)[:, :CHUNK]
        return value

    even = jnp.zeros((2 * rows, 2 * LANES), jnp.float32)
    half = jnp.zeros((2 * rows, 2 * LANES), jnp.float32)
    odd = jnp.zeros((4 * rows, 4 * LANES), jnp.float32)
    for g, end in enumerate(ends):
        for c in range(int(end) - GROUPS[g], int(end)):
            at = c * CHUNK
            x0, x1, x2, x3 = (window(m * QUARTER + at) for m in range(4))
            sum02, sum13 = x0 + x2, x1 + x3
            for target, first, value in (
                (y_even, 0, sum02 + sum13),
                (y_half, 0, sum02 - sum13),
                (y_odd, 0, x0 - x2),
                (y_odd, 2 * rows, x1 - x3),
            ):
                high, low = split(value)
                target[first : first + rows, at : at + CHUNK] = high
                target[first + rows : first + 2 * rows, at : at + CHUNK] = low
        copies[g].wait()
        lo, hi = int(end - GROUPS[g]) * CHUNK, int(end) * CHUNK
        even += jnp.dot(y_even[:, lo:hi], table[lo:hi, : 2 * LANES], preferred_element_type=jnp.float32)
        half += jnp.dot(y_half[:, lo:hi], table[lo:hi, 2 * LANES : 4 * LANES], preferred_element_type=jnp.float32)
        odd += jnp.dot(y_odd[:, lo:hi], table[lo:hi, 4 * LANES :], preferred_element_type=jnp.float32)

    even = even[:rows] + even[rows:]
    half = half[:rows] + half[rows:]
    u = odd[:rows] + odd[rows : 2 * rows]
    v = odd[2 * rows : 3 * rows] + odd[3 * rows :]
    pairs = (
        (even[:, :LANES], even[:, LANES:]),
        (half[:, :LANES], half[:, LANES:]),
        (u[:, :LANES] + v[:, LANES : 2 * LANES], u[:, LANES : 2 * LANES] - v[:, :LANES]),
        (u[:, 2 * LANES : 3 * LANES] - v[:, 3 * LANES :], u[:, 3 * LANES :] + v[:, 2 * LANES : 3 * LANES]),
    )
    power = [re * re + im * im for re, im in pairs]
    band_power = jnp.sum(power[0] + power[1] + power[2] + power[3], axis=1, keepdims=True) / NB
    pieces = []
    for (re, im), own in zip(pairs, power):
        scale = 1.0 / jnp.sqrt(own + water_level * band_power + 1e-06)
        pieces += [re * scale, im * scale]
    lanes = lax.broadcasted_iota(jnp.int32, (rows, LANES), 1)
    packed = []
    for p in range(7):
        moved = pltpu.roll(pieces[7], (PER - p * SPARE) % LANES, axis=1)
        packed.append(jnp.where(lanes < PER, pieces[p], moved))
    whitened = jnp.concatenate(packed, axis=1).astype(jnp.bfloat16)
    count_copy.wait()
    index_copy.wait()
    count = counts[lax.axis_index("chan")]
    source = lax.broadcasted_iota(jnp.int32, (rows, rows), 0)
    slot = lax.broadcasted_iota(jnp.int32, (rows, rows), 1)
    chosen = jnp.logical_and(source == index[...], slot < count)
    pick = jnp.where(chosen, 1.0, 0.0).astype(jnp.bfloat16)
    own = lax.dot_general(pick, whitened, (((0,), (0,)), ((), ())), preferred_element_type=jnp.float32)
    narrow = own.astype(jnp.bfloat16)
    out_ref[...] = narrow
    first_ref[...] = narrow[: rows // 2]
    second_ref[...] = narrow[rows // 2 :]
    weight_copy.wait()
    for lag in range(lag_share):
        lag_ref[lag * rows : (lag + 1) * rows, :] = (own * weights[lag : lag + 1, :]).astype(jnp.bfloat16)


def spectra(raw_rows, index_row, live_count, table, weights):
    rows = raw_rows.shape[0]
    lag_share = weights.shape[1]
    return pl.pallas_call(
        functools.partial(spectra_kernel, lag_share),
        out_shape=[
            pltpu.VMEM((rows, WIDTH), jnp.bfloat16),
            pltpu.VMEM((rows // 2, WIDTH), jnp.bfloat16),
            pltpu.VMEM((rows // 2, WIDTH), jnp.bfloat16),
            pltpu.VMEM((lag_share * rows, WIDTH), jnp.bfloat16),
        ],
        in_specs=[pl.BlockSpec(memory_space=pltpu.HBM)] * 5,
        out_specs=[pl.BlockSpec(memory_space=pltpu.VMEM)] * 4,
        scratch_shapes=[
            pltpu.VMEM((rows, S), jnp.bfloat16),
            pltpu.VMEM((rows, LANES), jnp.bfloat16),
            pltpu.VMEM((DEPTH, 8 * LANES), jnp.bfloat16),
            pltpu.VMEM((2 * rows, DEPTH), jnp.bfloat16),
            pltpu.VMEM((2 * rows, DEPTH), jnp.bfloat16),
            pltpu.VMEM((4 * rows, DEPTH), jnp.bfloat16),
            pltpu.SMEM(live_count.shape, jnp.int32),
            pltpu.VMEM(index_row.shape, jnp.int32),
            pltpu.VMEM(weights.shape[1:], jnp.float32),
            pltpu.SemaphoreType.DMA((3,)),
            pltpu.SemaphoreType.DMA((1 + len(GROUPS),)),
        ],
        compiler_params=pltpu.CompilerParams(vmem_limit_bytes=VMEM_KIB * 1024),
        cost_estimate=pl.CostEstimate(
            flops=2 * DEPTH * rows * 3072, bytes_accessed=DEPTH * 2048 + rows * S * 2, transcendentals=0
        ),
        name="spectra",
    )(*(pltpu.with_memory_space_constraint(a, pltpu.HBM) for a in (live_count, index_row, raw_rows, table, weights)))


def correlate(lag_rows, columns):
    product = lax.dot_general(
        lag_rows, columns, (((1,), (1,)), ((), ())), preferred_element_type=jnp.float32
    )
    return product.astype(jnp.bfloat16)


def put(out, product, plane, rows):
    at = pl.multiple_of(plane * 2 * rows, 2 * rows)
    for lag in range(out.shape[0]):
        out[lag, :, pl.ds(at, 2 * rows)] = product[lag * rows : (lag + 1) * rows]


def plane_products(lag_rows, tiles, x, rows):
    columns = jnp.concatenate([block for blocks in tiles for block in blocks], axis=0)
    both = lax.dot_general(lag_rows, columns, (((1,), (1,)), ((), ())), preferred_element_type=jnp.float32)
    products = [both[:, place * 2 * rows : (place + 1) * 2 * rows] for place in range(len(tiles))]
    return [jnp.where(x == 0, p, pltpu.roll(p, rows, axis=1)).astype(jnp.bfloat16) for p in products]


def early_kernel(lags, own, side, near, near_swap, out):
    x = lax.axis_index("chan") % 2
    upper = lax.axis_index("pair") == 1
    nearest = (
        jnp.where(upper, near_swap[...], near[...]),
        jnp.where(upper, near[...], near_swap[...]),
    )
    tiles = ((own[...], side[...]), nearest)
    for place, product in enumerate(plane_products(lags[...], tiles, x, own.shape[0])):
        out[place] = product


def late_kernel(lags, early, far, far_swap, cross_a, cross_b, cross_swap_a, cross_swap_b, out):
    me = lax.axis_index("chan")
    core = lax.axis_index("pair")
    x, z = me % 2, me // 2
    rows = far.shape[0]
    tiles = (
        (far[...], cross_swap_a[...], cross_swap_b[...]),
        (far_swap[...], cross_a[...], cross_b[...]),
    )
    put(out, early[0], z, rows)
    put(out, early[1], z ^ 1, rows)
    first, second = plane_products(lags[...], tiles, x, rows)
    put(out, first, z ^ (2 + core), rows)
    put(out, second, z ^ (3 - core), rows)


def exchange_eight(own, first, second, lags):
    def split_move(mask1, mask0):
        pairs = [(2 * c + 1, 2 * (c ^ mask1) + 1) for c in range(8)] + [(2 * c, 2 * (c ^ mask0)) for c in range(8)]
        return lambda a: lax.ppermute(a, ("chan", "pair"), pairs)

    def forward(a):
        pairs = [(2 * c + p, 2 * (c ^ 1) + 1 - p) for c in range(8) for p in range(2)]
        return lax.ppermute(a, ("chan", "pair"), pairs)

    def swap(a):
        return lax.ppermute(a, "pair", [(0, 1), (1, 0)])

    far_a = split_move(6, 4)(first)
    far_b = split_move(6, 4)(second)
    side = split_move(1, 1)(own)
    near = split_move(3, 2)(own)
    cross_a = forward(far_a)
    cross_b = forward(far_b)
    cross_swap_a = swap(cross_a)
    cross_b, cross_swap_a = lax.optimization_barrier((cross_b, cross_swap_a))
    far = jnp.concatenate([far_a, far_b], axis=0)
    far_swap = swap(far)
    near_swap = swap(near)
    cross_swap_b = swap(cross_b)
    lag_share, rows = lags.shape[0] // own.shape[0], own.shape[0]
    early = pl.pallas_call(
        early_kernel,
        out_shape=pltpu.VMEM((2, lag_share * rows, 2 * rows), jnp.bfloat16),
        in_specs=[pl.BlockSpec(memory_space=pltpu.VMEM)] * 5,
        out_specs=pl.BlockSpec(memory_space=pltpu.VMEM),
        compiler_params=pltpu.CompilerParams(vmem_limit_bytes=CORR_KIB * 1024),
        cost_estimate=pl.CostEstimate(
            flops=2 * lag_share * rows * 4 * rows * WIDTH, bytes_accessed=8 * rows * WIDTH * 2, transcendentals=0
        ),
        name="correlate_early",
    )(lags, own, side, near, near_swap)
    return pl.pallas_call(
        late_kernel,
        out_shape=jax.ShapeDtypeStruct((lag_share, rows, 8 * rows), jnp.bfloat16),
        in_specs=[pl.BlockSpec(memory_space=pltpu.VMEM)] * 8,
        out_specs=pl.BlockSpec(memory_space=pltpu.VMEM),
        compiler_params=pltpu.CompilerParams(vmem_limit_bytes=CORR_KIB * 1024),
        cost_estimate=pl.CostEstimate(
            flops=2 * lag_share * rows * 4 * rows * WIDTH, bytes_accessed=8 * rows * WIDTH * 2, transcendentals=0
        ),
        name="correlate_late",
    )(lags, early, far, far_swap, cross_a, cross_b, cross_swap_a, cross_swap_b)


def shards(table, weights, raw, live_index, live_count):
    slot_count, seg_count, samples = raw.shape
    pairs = lax.axis_size("pair")
    own, first, second, lags = spectra(
        raw.reshape(slot_count * seg_count, samples),
        live_index,
        live_count,
        table,
        weights.reshape(pairs, L // pairs, WIDTH),
    )
    if lax.axis_size("chan") == 8 and pairs == 2 and slot_count == 64:
        return exchange_eight(own, first, second, lags)
    product = correlate(lags, lax.all_gather(own, "chan", axis=0, tiled=True))
    return product.reshape(L // pairs, slot_count, -1)


def solution(mesh):
    local = functools.partial(shards, jnp.asarray(quarter_table()), jnp.asarray(lag_table()))
    return jax.shard_map(
        local,
        mesh=mesh,
        in_specs=(P(("groups", "chan"), None, None), P(("groups", "chan"), None), P("groups")),
        out_specs=P("pair", ("groups", "chan"), None),
        check_vma=False,
    )
```

```python
import functools

import jax
import jax.numpy as jnp
import numpy as np
from jax import lax
from jax.experimental import pallas as pl
from jax.experimental.pallas import tpu as pltpu
from jax.sharding import PartitionSpec as P

S = 12000
NB = 448
NSEG = 1
L = 6
LSTEP = 125
F0 = 60

water_level = 0.1

QUARTER = S // 4
CHUNK = 256
CHUNKS = -(-QUARTER // CHUNK)
DEPTH = CHUNKS * CHUNK
GROUPS = (2, 2, 2, 2, 2, 2)
RES = (0, 2, 1, 3)
PER = NB // 4
LANES = 128
SPARE = LANES - PER
WIDTH = 2 * NB
VMEM_KIB = 40 * 1024
CORR_KIB = 32 * 1024


def bins_of(residue):
    return np.arange(residue, NB, 4)


def quarter_table():
    table = np.zeros((DEPTH, 8 * LANES), np.float64)
    t = np.arange(QUARTER, dtype=np.int64)
    step = np.float64(np.float32(2.0 * np.pi / S))
    for place, residue in enumerate(RES):
        angles = (t[:, None] * (F0 + bins_of(residue))[None, :] % S) * step
        at = 2 * place * LANES
        table[:QUARTER, at : at + PER] = np.cos(angles)
        table[:QUARTER, at + LANES : at + LANES + PER] = -np.sin(angles)
    return table.astype(np.float32).astype(jnp.bfloat16)


def packed_bins():
    pieces = [bins_of(residue) for residue in RES for _ in range(2)]
    columns = []
    for p in range(7):
        columns.append(pieces[p])
        columns.append(pieces[7][p * SPARE : (p + 1) * SPARE])
    return np.concatenate(columns)


def lag_table():
    bins = packed_bins()
    taper = np.float32(0.5) - np.float32(0.5) * np.cos(
        np.float32(2.0 * np.pi) * (bins.astype(np.float32) + np.float32(0.5)) / np.float32(NB)
    )
    phase = (F0 + bins)[None, :] * (np.arange(L) * LSTEP)[:, None] % S
    waves = np.cos(phase.astype(np.float32) * np.float32(2.0 * np.pi / S))
    return (taper[None, :] * waves / np.sqrt(np.float32(NSEG * NB))).astype(np.float32)


def split(value):
    high = value.astype(jnp.bfloat16)
    low = (value - high.astype(jnp.float32)).astype(jnp.bfloat16)
    return high, low


def spectra_kernel(
    lag_share,
    count_ref,
    index_ref,
    raw_ref,
    table_ref,
    weight_ref,
    out_ref,
    first_ref,
    second_ref,
    lag_ref,
    x,
    tail,
    table,
    y_even,
    y_half,
    y_odd,
    counts,
    index,
    weights,
    small_sems,
    sems,
):
    rows = x.shape[0]
    whole = S // LANES * LANES
    x_copy = pltpu.make_async_copy(raw_ref, x, sems.at[0])
    x_copy.start()
    count_copy = pltpu.make_async_copy(count_ref, counts, small_sems.at[0])
    index_copy = pltpu.make_async_copy(index_ref, index, small_sems.at[1])
    count_copy.start()
    index_copy.start()
    weight_copy = pltpu.make_async_copy(weight_ref.at[lax.axis_index("pair")], weights, small_sems.at[2])
    weight_copy.start()
    copies = []
    ends = np.cumsum(GROUPS)
    for g, end in enumerate(ends):
        span = pl.ds(int(end - GROUPS[g]) * CHUNK, GROUPS[g] * CHUNK)
        copies.append(pltpu.make_async_copy(table_ref.at[span, :], table.at[span, :], sems.at[1 + g]))
        copies[-1].start()
    tail[...] = jnp.zeros_like(tail)
    x_copy.wait()
    tail[:, : S - whole] = x[:, whole:S]

    def window(start):
        base = start // LANES * LANES
        shift = start - base
        parts = []
        for lane in range(base, base + CHUNK + (LANES if shift else 0), LANES):
            if lane + LANES <= S:
                parts.append(x[:, lane : lane + LANES])
            elif lane < S:
                parts.append(tail[...])
            else:
                parts.append(jnp.zeros((rows, LANES), x.dtype))
        value = jnp.concatenate(parts, axis=1).astype(jnp.float32)
        if shift:
            value = pltpu.roll(value, value.shape[1] - shift, axis=1)[:, :CHUNK]
        return value

    even = jnp.zeros((2 * rows, 2 * LANES), jnp.float32)
    half = jnp.zeros((2 * rows, 2 * LANES), jnp.float32)
    odd = jnp.zeros((4 * rows, 4 * LANES), jnp.float32)
    for g, end in enumerate(ends):
        for c in range(int(end) - GROUPS[g], int(end)):
            at = c * CHUNK
            x0, x1, x2, x3 = (window(m * QUARTER + at) for m in range(4))
            sum02, sum13 = x0 + x2, x1 + x3
            for target, first, value in (
                (y_even, 0, sum02 + sum13),
                (y_half, 0, sum02 - sum13),
                (y_odd, 0, x0 - x2),
                (y_odd, 2 * rows, x1 - x3),
            ):
                high, low = split(value)
                target[first : first + rows, at : at + CHUNK] = high
                target[first + rows : first + 2 * rows, at : at + CHUNK] = low
        copies[g].wait()
        lo, hi = int(end - GROUPS[g]) * CHUNK, int(end) * CHUNK
        even += jnp.dot(y_even[:, lo:hi], table[lo:hi, : 2 * LANES], preferred_element_type=jnp.float32)
        half += jnp.dot(y_half[:, lo:hi], table[lo:hi, 2 * LANES : 4 * LANES], preferred_element_type=jnp.float32)
        odd += jnp.dot(y_odd[:, lo:hi], table[lo:hi, 4 * LANES :], preferred_element_type=jnp.float32)

    even = even[:rows] + even[rows:]
    half = half[:rows] + half[rows:]
    u = odd[:rows] + odd[rows : 2 * rows]
    v = odd[2 * rows : 3 * rows] + odd[3 * rows :]
    pairs = (
        (even[:, :LANES], even[:, LANES:]),
        (half[:, :LANES], half[:, LANES:]),
        (u[:, :LANES] + v[:, LANES : 2 * LANES], u[:, LANES : 2 * LANES] - v[:, :LANES]),
        (u[:, 2 * LANES : 3 * LANES] - v[:, 3 * LANES :], u[:, 3 * LANES :] + v[:, 2 * LANES : 3 * LANES]),
    )
    power = [re * re + im * im for re, im in pairs]
    band_power = jnp.sum(power[0] + power[1] + power[2] + power[3], axis=1, keepdims=True) / NB
    pieces = []
    for (re, im), own in zip(pairs, power):
        scale = 1.0 / jnp.sqrt(own + water_level * band_power + 1e-06)
        pieces += [re * scale, im * scale]
    lanes = lax.broadcasted_iota(jnp.int32, (rows, LANES), 1)
    packed = []
    for p in range(7):
        moved = pltpu.roll(pieces[7], (PER - p * SPARE) % LANES, axis=1)
        packed.append(jnp.where(lanes < PER, pieces[p], moved))
    whitened = jnp.concatenate(packed, axis=1).astype(jnp.bfloat16)
    count_copy.wait()
    index_copy.wait()
    count = counts[lax.axis_index("chan")]
    source = lax.broadcasted_iota(jnp.int32, (rows, rows), 0)
    slot = lax.broadcasted_iota(jnp.int32, (rows, rows), 1)
    chosen = jnp.logical_and(source == index[...], slot < count)
    pick = jnp.where(chosen, 1.0, 0.0).astype(jnp.bfloat16)
    own = lax.dot_general(pick, whitened, (((0,), (0,)), ((), ())), preferred_element_type=jnp.float32)
    narrow = own.astype(jnp.bfloat16)
    out_ref[...] = narrow
    first_ref[...] = narrow[: rows // 2]
    second_ref[...] = narrow[rows // 2 :]
    weight_copy.wait()
    for lag in range(lag_share):
        lag_ref[lag * rows : (lag + 1) * rows, :] = (own * weights[lag : lag + 1, :]).astype(jnp.bfloat16)


def spectra(raw_rows, index_row, live_count, table, weights):
    rows = raw_rows.shape[0]
    lag_share = weights.shape[1]
    return pl.pallas_call(
        functools.partial(spectra_kernel, lag_share),
        out_shape=[
            pltpu.VMEM((rows, WIDTH), jnp.bfloat16),
            pltpu.VMEM((rows // 2, WIDTH), jnp.bfloat16),
            pltpu.VMEM((rows // 2, WIDTH), jnp.bfloat16),
            pltpu.VMEM((lag_share * rows, WIDTH), jnp.bfloat16),
        ],
        in_specs=[pl.BlockSpec(memory_space=pltpu.HBM)] * 5,
        out_specs=[pl.BlockSpec(memory_space=pltpu.VMEM)] * 4,
        scratch_shapes=[
            pltpu.VMEM((rows, S), jnp.bfloat16),
            pltpu.VMEM((rows, LANES), jnp.bfloat16),
            pltpu.VMEM((DEPTH, 8 * LANES), jnp.bfloat16),
            pltpu.VMEM((2 * rows, DEPTH), jnp.bfloat16),
            pltpu.VMEM((2 * rows, DEPTH), jnp.bfloat16),
            pltpu.VMEM((4 * rows, DEPTH), jnp.bfloat16),
            pltpu.SMEM(live_count.shape, jnp.int32),
            pltpu.VMEM(index_row.shape, jnp.int32),
            pltpu.VMEM(weights.shape[1:], jnp.float32),
            pltpu.SemaphoreType.DMA((3,)),
            pltpu.SemaphoreType.DMA((1 + len(GROUPS),)),
        ],
        compiler_params=pltpu.CompilerParams(vmem_limit_bytes=VMEM_KIB * 1024),
        cost_estimate=pl.CostEstimate(
            flops=2 * DEPTH * rows * 3072, bytes_accessed=DEPTH * 2048 + rows * S * 2, transcendentals=0
        ),
        name="spectra",
    )(*(pltpu.with_memory_space_constraint(a, pltpu.HBM) for a in (live_count, index_row, raw_rows, table, weights)))


def correlate(lag_rows, columns):
    product = lax.dot_general(
        lag_rows, columns, (((1,), (1,)), ((), ())), preferred_element_type=jnp.float32
    )
    return product.astype(jnp.bfloat16)


def put(out, product, plane, rows):
    at = pl.multiple_of(plane * 2 * rows, 2 * rows)
    for lag in range(out.shape[0]):
        out[lag, :, pl.ds(at, 2 * rows)] = product[lag * rows : (lag + 1) * rows]


def plane_products(lag_rows, tiles, x, rows):
    columns = jnp.concatenate([block for blocks in tiles for block in blocks], axis=0)
    both = lax.dot_general(lag_rows, columns, (((1,), (1,)), ((), ())), preferred_element_type=jnp.float32)
    products = [both[:, place * 2 * rows : (place + 1) * 2 * rows] for place in range(len(tiles))]
    return [jnp.where(x == 0, p, pltpu.roll(p, rows, axis=1)).astype(jnp.bfloat16) for p in products]


def early_kernel(lags, own, side, near, near_swap, out):
    x = lax.axis_index("chan") % 2
    upper = lax.axis_index("pair") == 1
    nearest = (
        jnp.where(upper, near_swap[...], near[...]),
        jnp.where(upper, near[...], near_swap[...]),
    )
    tiles = ((own[...], side[...]), nearest)
    for place, product in enumerate(plane_products(lags[...], tiles, x, own.shape[0])):
        out[place] = product


def late_kernel(lags, early, far, far_swap, cross_a, cross_b, cross_swap_a, cross_swap_b, out):
    me = lax.axis_index("chan")
    core = lax.axis_index("pair")
    x, z = me % 2, me // 2
    rows = far.shape[0]
    tiles = (
        (far[...], cross_swap_a[...], cross_swap_b[...]),
        (far_swap[...], cross_a[...], cross_b[...]),
    )
    put(out, early[0], z, rows)
    put(out, early[1], z ^ 1, rows)
    first, second = plane_products(lags[...], tiles, x, rows)
    put(out, first, z ^ (2 + core), rows)
    put(out, second, z ^ (3 - core), rows)


def exchange_eight(own, first, second, lags):
    def split_move(mask1, mask0):
        pairs = [(2 * c + 1, 2 * (c ^ mask1) + 1) for c in range(8)] + [(2 * c, 2 * (c ^ mask0)) for c in range(8)]
        return lambda a: lax.ppermute(a, ("chan", "pair"), pairs)

    def cross_move(mask1, mask0):
        pairs = [(2 * c, 2 * (c ^ mask1) + 1) for c in range(8)] + [(2 * c + 1, 2 * (c ^ mask0)) for c in range(8)]
        return lambda a: lax.ppermute(a, ("chan", "pair"), pairs)

    def forward(a):
        pairs = [(2 * c + p, 2 * (c ^ 1) + 1 - p) for c in range(8) for p in range(2)]
        return lax.ppermute(a, ("chan", "pair"), pairs)

    def swap(a):
        return lax.ppermute(a, "pair", [(0, 1), (1, 0)])

    far_a = cross_move(6, 4)(first)
    far_b = cross_move(6, 4)(second)
    side = forward(own)
    near = split_move(3, 2)(own)
    cross_a = forward(far_a)
    cross_b = forward(far_b)
    cross_swap_a = swap(cross_a)
    cross_b, cross_swap_a = lax.optimization_barrier((cross_b, cross_swap_a))
    far = jnp.concatenate([far_a, far_b], axis=0)
    far_swap = swap(far)
    near_swap = swap(near)
    cross_swap_b = swap(cross_b)
    lag_share, rows = lags.shape[0] // own.shape[0], own.shape[0]
    early = pl.pallas_call(
        early_kernel,
        out_shape=pltpu.VMEM((2, lag_share * rows, 2 * rows), jnp.bfloat16),
        in_specs=[pl.BlockSpec(memory_space=pltpu.VMEM)] * 5,
        out_specs=pl.BlockSpec(memory_space=pltpu.VMEM),
        compiler_params=pltpu.CompilerParams(vmem_limit_bytes=CORR_KIB * 1024),
        cost_estimate=pl.CostEstimate(
            flops=2 * lag_share * rows * 4 * rows * WIDTH, bytes_accessed=8 * rows * WIDTH * 2, transcendentals=0
        ),
        name="correlate_early",
    )(lags, own, side, near, near_swap)
    return pl.pallas_call(
        late_kernel,
        out_shape=jax.ShapeDtypeStruct((lag_share, rows, 8 * rows), jnp.bfloat16),
        in_specs=[pl.BlockSpec(memory_space=pltpu.VMEM)] * 8,
        out_specs=pl.BlockSpec(memory_space=pltpu.VMEM),
        compiler_params=pltpu.CompilerParams(vmem_limit_bytes=CORR_KIB * 1024),
        cost_estimate=pl.CostEstimate(
            flops=2 * lag_share * rows * 4 * rows * WIDTH, bytes_accessed=8 * rows * WIDTH * 2, transcendentals=0
        ),
        name="correlate_late",
    )(lags, early, far, far_swap, cross_a, cross_b, cross_swap_a, cross_swap_b)


def shards(table, weights, raw, live_index, live_count):
    slot_count, seg_count, samples = raw.shape
    pairs = lax.axis_size("pair")
    own, first, second, lags = spectra(
        raw.reshape(slot_count * seg_count, samples),
        live_index,
        live_count,
        table,
        weights.reshape(pairs, L // pairs, WIDTH),
    )
    if lax.axis_size("chan") == 8 and pairs == 2 and slot_count == 64:
        return exchange_eight(own, first, second, lags)
    product = correlate(lags, lax.all_gather(own, "chan", axis=0, tiled=True))
    return product.reshape(L // pairs, slot_count, -1)


def solution(mesh):
    local = functools.partial(shards, jnp.asarray(quarter_table()), jnp.asarray(lag_table()))
    return jax.shard_map(
        local,
        mesh=mesh,
        in_specs=(P(("groups", "chan"), None, None), P(("groups", "chan"), None), P("groups")),
        out_specs=P("pair", ("groups", "chan"), None),
        check_vma=False,
    )
```

```python
import functools

import jax
import jax.numpy as jnp
import numpy as np
from jax import lax
from jax.experimental import pallas as pl
from jax.experimental.pallas import tpu as pltpu
from jax.sharding import PartitionSpec as P

S = 12000
NB = 448
NSEG = 1
L = 6
LSTEP = 125
F0 = 60

water_level = 0.1

QUARTER = S // 4
CHUNK = 256
CHUNKS = -(-QUARTER // CHUNK)
DEPTH = CHUNKS * CHUNK
GROUPS = (2, 2, 2, 2, 2, 2)
RES = (0, 2, 1, 3)
PER = NB // 4
LANES = 128
SPARE = LANES - PER
WIDTH = 2 * NB
VMEM_KIB = 40 * 1024
CORR_KIB = 32 * 1024


def bins_of(residue):
    return np.arange(residue, NB, 4)


def quarter_table():
    table = np.zeros((DEPTH, 8 * LANES), np.float64)
    t = np.arange(QUARTER, dtype=np.int64)
    step = np.float64(np.float32(2.0 * np.pi / S))
    for place, residue in enumerate(RES):
        angles = (t[:, None] * (F0 + bins_of(residue))[None, :] % S) * step
        at = 2 * place * LANES
        table[:QUARTER, at : at + PER] = np.cos(angles)
        table[:QUARTER, at + LANES : at + LANES + PER] = -np.sin(angles)
    return table.astype(np.float32).astype(jnp.bfloat16)


def packed_bins():
    pieces = [bins_of(residue) for residue in RES for _ in range(2)]
    columns = []
    for p in range(7):
        columns.append(pieces[p])
        columns.append(pieces[7][p * SPARE : (p + 1) * SPARE])
    return np.concatenate(columns)


def lag_table():
    bins = packed_bins()
    taper = np.float32(0.5) - np.float32(0.5) * np.cos(
        np.float32(2.0 * np.pi) * (bins.astype(np.float32) + np.float32(0.5)) / np.float32(NB)
    )
    phase = (F0 + bins)[None, :] * (np.arange(L) * LSTEP)[:, None] % S
    waves = np.cos(phase.astype(np.float32) * np.float32(2.0 * np.pi / S))
    return (taper[None, :] * waves / np.sqrt(np.float32(NSEG * NB))).astype(np.float32)


def split(value):
    high = value.astype(jnp.bfloat16)
    low = (value - high.astype(jnp.float32)).astype(jnp.bfloat16)
    return high, low


def spectra_kernel(
    count_ref,
    index_ref,
    raw_ref,
    table_ref,
    weight_ref,
    out_ref,
    first_ref,
    second_ref,
    weights,
    x,
    tail,
    table,
    y_even,
    y_half,
    y_odd,
    counts,
    index,
    small_sems,
    sems,
):
    rows = x.shape[0]
    whole = S // LANES * LANES
    x_copy = pltpu.make_async_copy(raw_ref, x, sems.at[0])
    x_copy.start()
    count_copy = pltpu.make_async_copy(count_ref, counts, small_sems.at[0])
    index_copy = pltpu.make_async_copy(index_ref, index, small_sems.at[1])
    count_copy.start()
    index_copy.start()
    weight_copy = pltpu.make_async_copy(weight_ref.at[lax.axis_index("pair")], weights, small_sems.at[2])
    weight_copy.start()
    copies = []
    ends = np.cumsum(GROUPS)
    for g, end in enumerate(ends):
        span = pl.ds(int(end - GROUPS[g]) * CHUNK, GROUPS[g] * CHUNK)
        copies.append(pltpu.make_async_copy(table_ref.at[span, :], table.at[span, :], sems.at[1 + g]))
        copies[-1].start()
    tail[...] = jnp.zeros_like(tail)
    x_copy.wait()
    tail[:, : S - whole] = x[:, whole:S]

    def window(start):
        base = start // LANES * LANES
        shift = start - base
        parts = []
        for lane in range(base, base + CHUNK + (LANES if shift else 0), LANES):
            if lane + LANES <= S:
                parts.append(x[:, lane : lane + LANES])
            elif lane < S:
                parts.append(tail[...])
            else:
                parts.append(jnp.zeros((rows, LANES), x.dtype))
        value = jnp.concatenate(parts, axis=1).astype(jnp.float32)
        if shift:
            value = pltpu.roll(value, value.shape[1] - shift, axis=1)[:, :CHUNK]
        return value

    even = jnp.zeros((2 * rows, 2 * LANES), jnp.float32)
    half = jnp.zeros((2 * rows, 2 * LANES), jnp.float32)
    odd = jnp.zeros((4 * rows, 4 * LANES), jnp.float32)
    for g, end in enumerate(ends):
        for c in range(int(end) - GROUPS[g], int(end)):
            at = c * CHUNK
            x0, x1, x2, x3 = (window(m * QUARTER + at) for m in range(4))
            sum02, sum13 = x0 + x2, x1 + x3
            for target, first, value in (
                (y_even, 0, sum02 + sum13),
                (y_half, 0, sum02 - sum13),
                (y_odd, 0, x0 - x2),
                (y_odd, 2 * rows, x1 - x3),
            ):
                high, low = split(value)
                target[first : first + rows, at : at + CHUNK] = high
                target[first + rows : first + 2 * rows, at : at + CHUNK] = low
        copies[g].wait()
        lo, hi = int(end - GROUPS[g]) * CHUNK, int(end) * CHUNK
        even += jnp.dot(y_even[:, lo:hi], table[lo:hi, : 2 * LANES], preferred_element_type=jnp.float32)
        half += jnp.dot(y_half[:, lo:hi], table[lo:hi, 2 * LANES : 4 * LANES], preferred_element_type=jnp.float32)
        odd += jnp.dot(y_odd[:, lo:hi], table[lo:hi, 4 * LANES :], preferred_element_type=jnp.float32)

    even = even[:rows] + even[rows:]
    half = half[:rows] + half[rows:]
    u = odd[:rows] + odd[rows : 2 * rows]
    v = odd[2 * rows : 3 * rows] + odd[3 * rows :]
    pairs = (
        (even[:, :LANES], even[:, LANES:]),
        (half[:, :LANES], half[:, LANES:]),
        (u[:, :LANES] + v[:, LANES : 2 * LANES], u[:, LANES : 2 * LANES] - v[:, :LANES]),
        (u[:, 2 * LANES : 3 * LANES] - v[:, 3 * LANES :], u[:, 3 * LANES :] + v[:, 2 * LANES : 3 * LANES]),
    )
    power = [re * re + im * im for re, im in pairs]
    band_power = jnp.sum(power[0] + power[1] + power[2] + power[3], axis=1, keepdims=True) / NB
    pieces = []
    for (re, im), own in zip(pairs, power):
        scale = 1.0 / jnp.sqrt(own + water_level * band_power + 1e-06)
        pieces += [re * scale, im * scale]
    lanes = lax.broadcasted_iota(jnp.int32, (rows, LANES), 1)
    packed = []
    for p in range(7):
        moved = pltpu.roll(pieces[7], (PER - p * SPARE) % LANES, axis=1)
        packed.append(jnp.where(lanes < PER, pieces[p], moved))
    whitened = jnp.concatenate(packed, axis=1).astype(jnp.bfloat16)
    count_copy.wait()
    index_copy.wait()
    count = counts[lax.axis_index("chan")]
    source = lax.broadcasted_iota(jnp.int32, (rows, rows), 0)
    slot = lax.broadcasted_iota(jnp.int32, (rows, rows), 1)
    chosen = jnp.logical_and(source == index[...], slot < count)
    pick = jnp.where(chosen, 1.0, 0.0).astype(jnp.bfloat16)
    own = lax.dot_general(pick, whitened, (((0,), (0,)), ((), ())), preferred_element_type=jnp.float32)
    narrow = own.astype(jnp.bfloat16)
    out_ref[...] = narrow
    first_ref[...] = narrow[: rows // 2]
    second_ref[...] = narrow[rows // 2 :]
    weight_copy.wait()


def spectra(raw_rows, index_row, live_count, table, weights):
    rows = raw_rows.shape[0]
    lag_share = weights.shape[1]
    return pl.pallas_call(
        spectra_kernel,
        out_shape=[
            pltpu.VMEM((rows, WIDTH), jnp.bfloat16),
            pltpu.VMEM((rows // 2, WIDTH), jnp.bfloat16),
            pltpu.VMEM((rows // 2, WIDTH), jnp.bfloat16),
            pltpu.VMEM((lag_share, WIDTH), jnp.float32),
        ],
        in_specs=[pl.BlockSpec(memory_space=pltpu.HBM)] * 5,
        out_specs=[pl.BlockSpec(memory_space=pltpu.VMEM)] * 4,
        scratch_shapes=[
            pltpu.VMEM((rows, S), jnp.bfloat16),
            pltpu.VMEM((rows, LANES), jnp.bfloat16),
            pltpu.VMEM((DEPTH, 8 * LANES), jnp.bfloat16),
            pltpu.VMEM((2 * rows, DEPTH), jnp.bfloat16),
            pltpu.VMEM((2 * rows, DEPTH), jnp.bfloat16),
            pltpu.VMEM((4 * rows, DEPTH), jnp.bfloat16),
            pltpu.SMEM(live_count.shape, jnp.int32),
            pltpu.VMEM(index_row.shape, jnp.int32),
            pltpu.SemaphoreType.DMA((3,)),
            pltpu.SemaphoreType.DMA((1 + len(GROUPS),)),
        ],
        compiler_params=pltpu.CompilerParams(vmem_limit_bytes=VMEM_KIB * 1024),
        cost_estimate=pl.CostEstimate(
            flops=2 * DEPTH * rows * 3072, bytes_accessed=DEPTH * 2048 + rows * S * 2, transcendentals=0
        ),
        name="spectra",
    )(*(pltpu.with_memory_space_constraint(a, pltpu.HBM) for a in (live_count, index_row, raw_rows, table, weights)))


def correlate(lag_rows, columns):
    product = lax.dot_general(
        lag_rows, columns, (((1,), (1,)), ((), ())), preferred_element_type=jnp.float32
    )
    return product.astype(jnp.bfloat16)


def put(out, product, plane, rows):
    at = pl.multiple_of(plane * 2 * rows, 2 * rows)
    for lag in range(out.shape[0]):
        out[lag, :, pl.ds(at, 2 * rows)] = product[lag * rows : (lag + 1) * rows]


def plane_products(lag_rows, tiles, x, rows):
    columns = jnp.concatenate([block for blocks in tiles for block in blocks], axis=0)
    both = lax.dot_general(lag_rows, columns, (((1,), (1,)), ((), ())), preferred_element_type=jnp.float32)
    products = [both[:, place * 2 * rows : (place + 1) * 2 * rows] for place in range(len(tiles))]
    return [jnp.where(x == 0, p, pltpu.roll(p, rows, axis=1)).astype(jnp.bfloat16) for p in products]


def early_kernel(weights, own, side, near, near_swap, out, lags):
    rows = own.shape[0]
    wide = own[...].astype(jnp.float32)
    for lag in range(weights.shape[0]):
        lags[lag * rows : (lag + 1) * rows, :] = (wide * weights[lag : lag + 1, :]).astype(jnp.bfloat16)
    x = lax.axis_index("chan") % 2
    upper = lax.axis_index("pair") == 1
    nearest = (
        jnp.where(upper, near_swap[...], near[...]),
        jnp.where(upper, near[...], near_swap[...]),
    )
    tiles = ((own[...], side[...]), nearest)
    for place, product in enumerate(plane_products(lags[...], tiles, x, own.shape[0])):
        out[place] = product


def late_kernel(lags, early, far, far_swap, cross_a, cross_b, cross_swap_a, cross_swap_b, out):
    me = lax.axis_index("chan")
    core = lax.axis_index("pair")
    x, z = me % 2, me // 2
    rows = far.shape[0]
    tiles = (
        (far[...], cross_swap_a[...], cross_swap_b[...]),
        (far_swap[...], cross_a[...], cross_b[...]),
    )
    put(out, early[0], z, rows)
    put(out, early[1], z ^ 1, rows)
    first, second = plane_products(lags[...], tiles, x, rows)
    put(out, first, z ^ (2 + core), rows)
    put(out, second, z ^ (3 - core), rows)


def exchange_eight(own, first, second, own_weights):
    def split_move(mask1, mask0):
        pairs = [(2 * c + 1, 2 * (c ^ mask1) + 1) for c in range(8)] + [(2 * c, 2 * (c ^ mask0)) for c in range(8)]
        return lambda a: lax.ppermute(a, ("chan", "pair"), pairs)

    def cross_move(mask1, mask0):
        pairs = [(2 * c, 2 * (c ^ mask1) + 1) for c in range(8)] + [(2 * c + 1, 2 * (c ^ mask0)) for c in range(8)]
        return lambda a: lax.ppermute(a, ("chan", "pair"), pairs)

    def forward(a):
        pairs = [(2 * c + p, 2 * (c ^ 1) + 1 - p) for c in range(8) for p in range(2)]
        return lax.ppermute(a, ("chan", "pair"), pairs)

    def swap(a):
        return lax.ppermute(a, "pair", [(0, 1), (1, 0)])

    far_a = cross_move(6, 4)(first)
    far_b = cross_move(6, 4)(second)
    side = forward(own)
    near = split_move(3, 2)(own)
    cross_a = forward(far_a)
    cross_b = forward(far_b)
    cross_swap_a = swap(cross_a)
    cross_b, cross_swap_a = lax.optimization_barrier((cross_b, cross_swap_a))
    far = jnp.concatenate([far_a, far_b], axis=0)
    far_swap = swap(far)
    near_swap = swap(near)
    cross_swap_b = swap(cross_b)
    lag_share, rows = own_weights.shape[0], own.shape[0]
    early, lags = pl.pallas_call(
        early_kernel,
        out_shape=[
            pltpu.VMEM((2, lag_share * rows, 2 * rows), jnp.bfloat16),
            pltpu.VMEM((lag_share * rows, WIDTH), jnp.bfloat16),
        ],
        in_specs=[pl.BlockSpec(memory_space=pltpu.VMEM)] * 5,
        out_specs=[pl.BlockSpec(memory_space=pltpu.VMEM)] * 2,
        compiler_params=pltpu.CompilerParams(vmem_limit_bytes=CORR_KIB * 1024),
        cost_estimate=pl.CostEstimate(
            flops=2 * lag_share * rows * 4 * rows * WIDTH, bytes_accessed=8 * rows * WIDTH * 2, transcendentals=0
        ),
        name="correlate_early",
    )(own_weights, own, side, near, near_swap)
    return pl.pallas_call(
        late_kernel,
        out_shape=jax.ShapeDtypeStruct((lag_share, rows, 8 * rows), jnp.bfloat16),
        in_specs=[pl.BlockSpec(memory_space=pltpu.VMEM)] * 8,
        out_specs=pl.BlockSpec(memory_space=pltpu.VMEM),
        compiler_params=pltpu.CompilerParams(vmem_limit_bytes=CORR_KIB * 1024),
        cost_estimate=pl.CostEstimate(
            flops=2 * lag_share * rows * 4 * rows * WIDTH, bytes_accessed=8 * rows * WIDTH * 2, transcendentals=0
        ),
        name="correlate_late",
    )(lags, early, far, far_swap, cross_a, cross_b, cross_swap_a, cross_swap_b)


def shards(table, weights, raw, live_index, live_count):
    slot_count, seg_count, samples = raw.shape
    pairs = lax.axis_size("pair")
    own, first, second, own_weights = spectra(
        raw.reshape(slot_count * seg_count, samples),
        live_index,
        live_count,
        table,
        weights.reshape(pairs, L // pairs, WIDTH),
    )
    if lax.axis_size("chan") == 8 and pairs == 2 and slot_count == 64:
        return exchange_eight(own, first, second, own_weights)
    lags = (own.astype(jnp.float32)[None] * own_weights[:, None, :]).astype(jnp.bfloat16).reshape(-1, WIDTH)
    product = correlate(lags, lax.all_gather(own, "chan", axis=0, tiled=True))
    return product.reshape(L // pairs, slot_count, -1)


def solution(mesh):
    local = functools.partial(shards, jnp.asarray(quarter_table()), jnp.asarray(lag_table()))
    return jax.shard_map(
        local,
        mesh=mesh,
        in_specs=(P(("groups", "chan"), None, None), P(("groups", "chan"), None), P("groups")),
        out_specs=P("pair", ("groups", "chan"), None),
        check_vma=False,
    )
```
